32 devices in a mesh: sec: 4 (over y, x), strip: 8 (over z, core).
Axes of the slice: x: 2, y: 2, z: 4, core: 2. Of those that a mesh axis runs over, the one named last changes fastest.
Arguments:
- image: bfloat16 [4, 16, 160, 160], P('sec', 'strip'), may hold values from -6 to 6
- peaks: int32 [4, 16, 2], P('sec', 'strip'), may hold values from 0 to 159
- row_source: int32 [4, 16, 160], P('sec', 'strip'), may hold values from 0 to 159
- row_weight: float32 [4, 16, 160], P('sec', 'strip'), may hold values from 0 to 1
- col_source: int32 [4, 16, 160], P('sec', 'strip'), may hold values from 0 to 159
- col_weight: float32 [4, 16, 160], P('sec', 'strip'), may hold values from 0 to 1
- owner: int32 [4, 2560, 1], P('sec', 'strip'), may hold values from 0 to 7; in each aligned block of 320 rows (0 to 319, 320 to 639, ..., all dimensions but the last counted through in order) at most 160 rows name the same one
- render_row: int32 [4, 2560], P('sec', 'strip'), may hold values from 0 to 319
Outputs:
- render: bfloat16 [4, 2560, 160], P('sec', 'strip')
- corr_map: float32 [4, 16, 160, 160], P('sec', 'strip')
The draws below stay inside these ranges and needn't reach their ends.
Inputs may be any that keep to these rules, and one draw needn't show every extreme that they name: Among the 320 tile rows of one strip, at most 160 have any one owner; in every draw some strip sends exactly 160 to some owner.
All inputs are finite; a program needn't handle non-finite values.
Results may differ from the reference program's by a relative error of at most 0.012.
Values may be sent and summed in bfloat16 or wider, within the bound.
No kernel may reach another device: no remote copies, remote signals or barrier semaphores. Data moves between devices by JAX's collectives and lax.ppermute only.
A program may use at most 64 MiB of HBM per device.

```python
import math
import jax
import jax.numpy as jnp
import numpy as np
from jax import lax

PS = 160
GC = 2
SECS = 4
P_DEV = 2
PATCHES = 16
TROWS = 2560
RROWS_DEV = 320
RROWS = 2560
CAP = 160
N_STRIP = 8


def set_ends(values, key, smallest, largest):
    spot = [jax.random.randint(jax.random.fold_in(key, axis), (), 0, length) for axis, length in enumerate(values.shape)]
    main_axis = values.shape.index(max(values.shape))
    next_to = spot[:main_axis] + [(spot[main_axis] + 1) % values.shape[main_axis]] + spot[main_axis + 1:]
    return values.at[tuple(spot)].set(smallest).at[tuple(next_to)].set(largest)


def block_levels(rng, dims, cuts, smallest, top_value):
    level = 1.0
    for position, shards_of in cuts:
        draws = jax.random.uniform(jax.random.fold_in(jax.random.fold_in(rng, 6), position), (shards_of,), jnp.float32, smallest / len(cuts), top_value / len(cuts))
        level = level * jnp.repeat(jnp.exp(draws), dims[position] // shards_of).reshape((-1,) + (1,) * (len(dims) - 1 - position))
    return level


def shared_out(stream_key, own, number, rows, count, top, reach, lean):
    order = jax.random.permutation(stream_key, count)
    crowded, common = load_shares(count, rows * top, reach, lean, True), load_shares(count, rows * top, reach, lean, False)
    places = jnp.arange(count)

    def named(sizes, rotation):
        used = int((sizes > 0).sum())
        fixed = max(1, used // 4)
        shifted = fixed + (places - fixed + rotation * (used - fixed)) % max(1, count - fixed)
        return jnp.zeros((count,), jnp.int32).at[order[jnp.where(places < fixed, places, shifted)]].set(jnp.asarray(sizes, jnp.int32))

    sizes = jnp.where(number % 4 == 0, named(crowded, number // 4), named(common, number - number // 4 - 1))
    mixed = jax.random.permutation(jax.random.fold_in(own, 3), count)
    donor, receiver = mixed[0:count // 2 * 2:2], mixed[1:count // 2 * 2:2]
    room = jnp.minimum(sizes[donor] - 1, reach - sizes[receiver]) // 2
    room = jnp.where((donor == order[0]) | (receiver == order[0]) | (sizes[receiver] == 0), 0, jnp.maximum(room, 0))
    shifted = jax.random.randint(jax.random.fold_in(own, 4), (count // 2,), 0, 1 << 20) % (room + 1)
    sizes = sizes.at[donor].add(-shifted).at[receiver].add(shifted)
    items = jnp.searchsorted(jnp.cumsum(sizes), jnp.arange(rows * top), side="right").astype(jnp.int32)
    grid = items.reshape(top, rows).T
    grid = grid[jax.random.permutation(jax.random.fold_in(own, 1), rows)]
    rotation = jax.random.randint(jax.random.fold_in(own, 2), (rows, 1), 0, top)
    return jnp.take_along_axis(grid, (jnp.arange(top)[None, :] + rotation) % top, axis=1)


def load_shares(count, total, most, slope, full):
    portions = [(1 << 20) // math.isqrt(grade ** slope) + 1 for grade in range(1, count + 1)]
    largest = most if full else min(most, max(-(-total // count), total * portions[0] // sum(portions)))
    least = 1 if total - largest >= count - 1 else 0
    given, spare = [largest] + [least] * (count - 1), total - largest - least * (count - 1)
    while spare > 0:
        candidates = [i for i in range(1, count) if given[i] < largest] or [i for i in range(1, count) if given[i] < most]
        mass, left = sum([portions[i] for i in candidates]), spare
        for i in candidates:
            more = min(most - given[i], max(1, left * portions[i] // mass), spare)
            given[i] = given[i] + more
            spare = spare - more
    return np.array(given)


def normal_values(own_key, dims, spread, most, cuts=(), kind=jnp.bfloat16):
    values = jax.random.normal(own_key, dims, jnp.float32) * spread
    if len(cuts) > 0:
        values = block_levels(own_key, dims, cuts, -0.22, 0.18) * values
    return jnp.clip(values, min=-most, max=most).astype(kind)


def setup_inputs(seed: int = 0) -> dict:
    arg_keys = jax.random.split(jax.random.key(seed), 9)
    image = normal_values(arg_keys[0], (SECS, PATCHES, PS, PS), 1.0, 6.0, ((0, 4), (1, 8)))
    peaks = set_ends(jax.random.randint(arg_keys[1], (SECS, PATCHES, 2), 0, PS), jax.random.fold_in(arg_keys[1], 1), 0, PS - 1).astype(jnp.int32)
    row_source = set_ends(jax.random.randint(arg_keys[2], (SECS, PATCHES, PS), 0, PS), jax.random.fold_in(arg_keys[2], 1), 0, PS - 1).astype(jnp.int32)
    row_weight = jnp.clip(1.0 * jax.random.uniform(arg_keys[3], (SECS, PATCHES, PS), jnp.float32) ** block_levels(arg_keys[3], (SECS, PATCHES, PS), ((0, 4), (1, 8)), -0.2, 0.2), 0.0, 1.0)
    col_source = set_ends(jax.random.randint(arg_keys[4], (SECS, PATCHES, PS), 0, PS), jax.random.fold_in(arg_keys[4], 1), 0, PS - 1).astype(jnp.int32)
    col_weight = jnp.clip(1.0 * jax.random.uniform(arg_keys[5], (SECS, PATCHES, PS), jnp.float32) ** block_levels(arg_keys[5], (SECS, PATCHES, PS), ((0, 4), (1, 8)), -0.2, 0.2), 0.0, 1.0)
    owner_keys = jax.random.split(jax.random.fold_in(arg_keys[6], 1), SECS * TROWS // (P_DEV * PS))
    owner_turns = jax.random.permutation(jax.random.fold_in(arg_keys[6], 3), SECS * TROWS // (P_DEV * PS))
    owner = jax.vmap(lambda own, number: shared_out(jax.random.fold_in(arg_keys[6], 2), own, number, P_DEV * PS, N_STRIP, 1, CAP, 1))(owner_keys, owner_turns).reshape((SECS, TROWS, 1))
    render_row = set_ends(jax.random.randint(arg_keys[7], (SECS, TROWS), 0, RROWS_DEV), jax.random.fold_in(arg_keys[7], 1), 0, RROWS_DEV - 1).astype(jnp.int32)
    return dict(image=image, peaks=peaks, row_source=row_source, row_weight=row_weight, col_source=col_source, col_weight=col_weight, owner=owner, render_row=render_row)


TWO_PI = 2.0 * 3.141592653589793


def product(form, left, right):
    return jnp.einsum(form, left.astype(jnp.float32), right.astype(jnp.float32))


def dft_tables(edge_len):
    positions = jnp.arange(edge_len, dtype=jnp.int32)
    phases = (positions[:, None] * positions[None, :]) % edge_len
    angles = phases.astype(jnp.float32) * (TWO_PI / edge_len)
    return jnp.cos(angles).astype(jnp.bfloat16), jnp.sin(angles).astype(jnp.bfloat16)


def spectrum(pixels, dft_cos, dft_sin):
    half_re = product("pyx,xv->pyv", pixels, dft_cos).astype(jnp.bfloat16)
    half_im = (-product("pyx,xv->pyv", pixels, dft_sin)).astype(jnp.bfloat16)
    spec_re = product("uy,pyv->puv", dft_cos, half_re) + product("uy,pyv->puv", dft_sin, half_im)
    spec_im = product("uy,pyv->puv", dft_cos, half_im) - product("uy,pyv->puv", dft_sin, half_re)
    return spec_re, spec_im


def surface(cross_re, cross_im, dft_cos, dft_sin, edge_len):
    back_re = (product("puv,vb->pub", cross_re, dft_cos) - product("puv,vb->pub", cross_im, dft_sin)).astype(jnp.bfloat16)
    back_im = (product("puv,vb->pub", cross_re, dft_sin) + product("puv,vb->pub", cross_im, dft_cos)).astype(jnp.bfloat16)
    inv_area = 1.0 / (edge_len * edge_len)
    return inv_area * (product("ua,pub->pab", dft_cos, back_re) - product("ua,pub->pab", dft_sin, back_im))


def peak_flow(corr, peak_pos, edge_len):
    patch_count = corr.shape[0]
    shifts = jnp.array([-1, 0, 1], dtype=jnp.int32)
    row_index = (peak_pos[:, 0][:, None] + shifts[None, :]) % edge_len
    picked = jnp.take_along_axis(corr, jnp.broadcast_to(row_index[:, :, None], (patch_count, 3, edge_len)), axis=1)
    col_center = jnp.broadcast_to((peak_pos[:, 1] % edge_len)[:, None, None], (patch_count, 3, 1))
    along_y = jnp.take_along_axis(picked, col_center, axis=2)[:, :, 0]
    col_index = (peak_pos[:, 1][:, None] + shifts[None, :]) % edge_len
    along_x = jnp.take_along_axis(picked[:, 1, :], col_index, axis=1)
    flow_y = (along_y[:, 2] - along_y[:, 0]) / (jnp.abs(along_y[:, 2]) + jnp.abs(along_y[:, 1]) + jnp.abs(along_y[:, 0]) + 1.0)
    flow_x = (along_x[:, 2] - along_x[:, 0]) / (jnp.abs(along_x[:, 2]) + jnp.abs(along_x[:, 1]) + jnp.abs(along_x[:, 0]) + 1.0)
    return flow_y, flow_x


def smooth_flow(flow):
    flow_grid = flow.reshape(-1, GC)
    padded = jnp.pad(flow_grid, ((0, 0), (1, 1)))
    return (0.5 * flow_grid + 0.25 * (padded[:, :-2] + padded[:, 2:])).reshape(-1)


def warp_matrix(sources, weights, edge_len):
    positions = jnp.arange(edge_len, dtype=jnp.int32)
    at_source = (positions[None, None, :] == sources[:, :, None]).astype(jnp.float32)
    at_next = (positions[None, None, :] == ((sources + 1) % edge_len)[:, :, None]).astype(jnp.float32)
    return (weights[:, :, None] * at_source + (1.0 - weights[:, :, None]) * at_next).astype(jnp.bfloat16)


def align_patches(pixels, prior, peak_pos, row_src, row_wt, col_src, col_wt, dft_cos, dft_sin):
    edge_len = pixels.shape[-1]
    ref_re, ref_im = spectrum(prior, dft_cos, dft_sin)
    img_re, img_im = spectrum(pixels, dft_cos, dft_sin)
    cross_re = (ref_re * img_re + ref_im * img_im).astype(jnp.bfloat16)
    cross_im = (ref_im * img_re - ref_re * img_im).astype(jnp.bfloat16)
    corr = surface(cross_re, cross_im, dft_cos, dft_sin, edge_len)
    flow_y, flow_x = peak_flow(corr, peak_pos, edge_len)
    smooth_y = smooth_flow(flow_y)
    smooth_x = smooth_flow(flow_x)
    row_mat = warp_matrix(row_src, row_wt, edge_len)
    col_mat = warp_matrix(col_src, col_wt, edge_len)
    row_warped = product("pyr,prx->pyx", row_mat, pixels).astype(jnp.bfloat16)
    warped_base = product("pyc,pxc->pyx", row_warped, col_mat)
    grad_y = 0.5 * (jnp.roll(warped_base, -1, axis=1) - jnp.roll(warped_base, 1, axis=1))
    grad_x = 0.5 * (jnp.roll(warped_base, -1, axis=2) - jnp.roll(warped_base, 1, axis=2))
    aligned = (warped_base + smooth_y[:, None, None] * grad_y + smooth_x[:, None, None] * grad_x).astype(jnp.bfloat16)
    return aligned, corr / edge_len


def render_section(aligned, owners_sec, target_rows):
    tile_rows = aligned.reshape(TROWS, PS).astype(jnp.float32)
    targets = owners_sec * RROWS_DEV + target_rows
    row_sums = jnp.zeros((RROWS, PS), jnp.float32).at[targets].add(tile_rows)
    counts = jnp.zeros((RROWS,), jnp.float32).at[targets].add(1.0)
    return (row_sums / jnp.maximum(counts, 1.0)[:, None]).astype(jnp.bfloat16)


def reference(image, peaks, row_source, row_weight, col_source, col_weight, owner, render_row):
    dft_cos, dft_sin = dft_tables(PS)

    def blocked(values_in):
        return values_in.reshape((N_STRIP, P_DEV) + values_in.shape[1:])

    def align_block(inputs):
        return align_patches(inputs[0], inputs[1], inputs[2], inputs[3], inputs[4], inputs[5], inputs[6], dft_cos, dft_sin)

    prior_sec = jnp.zeros((PATCHES, PS, PS), jnp.bfloat16)
    renders = []
    surfaces = []
    for section in range(SECS):
        pieces = (blocked(image[section]), blocked(prior_sec), blocked(peaks[section]), blocked(row_source[section]), blocked(row_weight[section]), blocked(col_source[section]), blocked(col_weight[section]))
        aligned_blocks, surface_blocks = lax.map(align_block, pieces)
        aligned = aligned_blocks.reshape(PATCHES, PS, PS)
        surfaces.append(surface_blocks.reshape(PATCHES, PS, PS))
        renders.append(render_section(aligned, owner[section, :, 0], render_row[section]))
        prior_sec = aligned
    return (jnp.stack(renders), jnp.stack(surfaces))
```

```python
import functools

import jax
import jax.numpy as jnp
import numpy as np
from jax import lax
from jax.experimental import pallas as pl
from jax.experimental.pallas import tpu as pltpu
from jax.sharding import PartitionSpec as P

GC = 2
LANES = 128
TWO_PI = 2.0 * 3.141592653589793
F32 = jnp.float32
BF16 = jnp.bfloat16
VMEM_BYTES = 40 * 1024 * 1024


def product(left, right):
    return jnp.dot(left, right, preferred_element_type=F32)


def dft_tables(edge):
    positions = np.arange(edge, dtype=np.int32)
    phases = positions[:, None] * positions[None, :] % edge
    angles = phases.astype(np.float32) * np.float32(TWO_PI / edge)
    return jnp.asarray(np.cos(angles), BF16), jnp.asarray(np.sin(angles), BF16)


def round_up(size, unit):
    return -(-size // unit) * unit


def message_rows(rows):
    return rows + rows // 4 + 16


def call(kernel, out_shape, n_in, smem=(), scratch=(), flops=1000000):
    specs = [
        pl.BlockSpec(memory_space=pltpu.SMEM if i in smem else pltpu.VMEM) for i in range(n_in)
    ]
    outs = jax.tree.map(lambda _: pl.BlockSpec(memory_space=pltpu.VMEM), out_shape)
    return pl.pallas_call(
        kernel,
        out_shape=out_shape,
        in_specs=specs,
        out_specs=outs,
        scratch_shapes=list(scratch),
        compiler_params=pltpu.CompilerParams(vmem_limit_bytes=VMEM_BYTES),
        cost_estimate=pl.CostEstimate(flops=flops, bytes_accessed=500000, transcendentals=0),
    )


def warp_matrix_t(source, weight, edge):
    spots = lax.broadcasted_iota(jnp.int32, (edge, edge), 0)
    following = jnp.where(source == edge - 1, 0, source + 1)
    first = jnp.where(spots == source, weight, 0.0)
    second = jnp.where(spots == following, 1.0 - weight, 0.0)
    return (first + second).astype(BF16)


def base_kernel(
    image_ref, row_src, row_wt, col_src, col_wt, owner_ref, target_ref, out_ref, keys
):
    count, edge, _ = image_ref.shape
    rows = count * edge
    part = rows // 4
    rest = edge - LANES
    pieces = []
    for p in range(count):
        row_t = warp_matrix_t(row_src[p : p + 1, :], row_wt[p : p + 1, :], edge)
        col_t = warp_matrix_t(col_src[p : p + 1, :], col_wt[p : p + 1, :], edge)
        row_warped = lax.dot_general(
            row_t, image_ref[p], (((0,), (0,)), ((), ())), preferred_element_type=F32
        ).astype(BF16)
        base = product(row_warped, col_t)
        out_ref[p * edge : (p + 1) * edge, :] = base[:, :LANES].astype(BF16)
        right = base[:, LANES:]
        pieces += [right[:part], right[part:]]
    out_ref[rows : rows + part, :] = jnp.concatenate(pieces, axis=1).astype(BF16)
    key = owner_ref[...] * rows + target_ref[...]
    keys[...] = jnp.full(keys.shape, -1.0, F32)
    keys[0:1, 0:rows] = (key >> 8).astype(F32)
    keys[8:9, 0:rows] = (key & 255).astype(F32)
    wide = keys.shape[1] // LANES
    blank = jnp.full((8 - wide, LANES), -1.0, F32)
    lines = []
    for half in (0, 8):
        lines += [keys[half : half + 1, j * LANES : (j + 1) * LANES] for j in range(wide)]
        lines += [blank]
    out_ref[rows + part :, :] = jnp.concatenate(lines, axis=0).astype(BF16)


def spectrum_of(pixels, dft_cos, dft_sin, count, edge):
    half_re = product(pixels, dft_cos).astype(BF16)
    half_im = (-product(pixels, dft_sin)).astype(BF16)
    spectra = []
    for p in range(count):
        h_re = half_re[p * edge : (p + 1) * edge]
        h_im = half_im[p * edge : (p + 1) * edge]
        spectra.append(
            (
                product(dft_cos, h_re) + product(dft_sin, h_im),
                product(dft_cos, h_im) - product(dft_sin, h_re),
            )
        )
    return spectra


def spectrum_kernel(image_ref, cos_ref, sin_ref, re_ref, im_ref):
    count, edge, _ = image_ref.shape
    pixels = image_ref[...].reshape(count * edge, edge)
    spectra = spectrum_of(pixels, cos_ref[...], sin_ref[...], count, edge)
    for p, (s_re, s_im) in enumerate(spectra):
        re_ref[p] = s_re
        im_ref[p] = s_im


def surface_kernel(
    message_ref, im_re_ref, im_im_ref, cos_ref, sin_ref, peaks_ref, corr_ref, near_ref, wrapped
):
    count, edge, _ = im_re_ref.shape
    rows = count * edge
    part = rows // 4
    rest = edge - LANES
    dft_cos, dft_sin = cos_ref[...], sin_ref[...]
    side = message_ref[rows : rows + part, :].astype(F32)
    groups = []
    for g in range(4):
        left = message_ref[g * part : (g + 1) * part, :].astype(F32)
        groups.append(jnp.concatenate([left, side[:, g * rest : (g + 1) * rest]], axis=1))
    pixels = jnp.concatenate(groups, axis=0)
    pixels = jnp.where(lax.axis_index("sec") > 0, pixels, 0.0).astype(BF16)
    spectra = spectrum_of(pixels, dft_cos, dft_sin, count, edge)
    lane = lax.broadcasted_iota(jnp.int32, (1, edge), 1)
    out_lane = lax.broadcasted_iota(jnp.int32, (8, LANES), 1)
    near = jnp.zeros((8, LANES), F32)
    for p, (ref_re, ref_im) in enumerate(spectra):
        img_re, img_im = im_re_ref[p], im_im_ref[p]
        cross_re = (ref_re * img_re + ref_im * img_im).astype(BF16)
        cross_im = (ref_im * img_re - ref_re * img_im).astype(BF16)
        back_re = (product(cross_re, dft_cos) - product(cross_im, dft_sin)).astype(BF16)
        back_im = (product(cross_re, dft_sin) + product(cross_im, dft_cos)).astype(BF16)
        corr = (product(dft_cos, back_re) - product(dft_sin, back_im)) * (1.0 / (edge * edge))
        corr_ref[p] = corr
        wrapped[p, 0:edge, :] = corr
        wrapped[p, edge : edge + 8, :] = corr[0:8]
        top = peaks_ref[p, 0] + (edge - 2)
        top = jnp.where(top >= edge, top - edge, top)
        eighth = pl.multiple_of((top >> 3) * 8, 8)
        tile = pltpu.roll(wrapped[p, pl.ds(eighth, 16), :], 16 - (top & 7), 0)[0:8]
        for j in range(5):
            spot = peaks_ref[p, 1] + (j - 2)
            spot = jnp.where(spot < 0, spot + edge, jnp.where(spot >= edge, spot - edge, spot))
            column = jnp.sum(jnp.where(lane == spot, tile, 0.0), axis=1, keepdims=True)
            near = jnp.where(out_lane == 8 * p + j, column, near)
    near_ref[...] = near


def chain_kernel(count, steps, *refs):
    near_refs, (smooth_ref, prior_ref) = refs[:steps], refs[steps:]
    section = lax.axis_index("sec")
    strip = lax.axis_index("strip")
    row = lax.broadcasted_iota(jnp.int32, (8, LANES), 0)
    lane = lax.broadcasted_iota(jnp.int32, (8, LANES), 1)

    def spread(values):
        tile = jnp.broadcast_to(values[0], (8, LANES))
        for p in range(1, count):
            tile = jnp.where(lane >= 8 * p, values[p], tile)
        return tile

    zeros = [jnp.zeros((1, 1), F32)] * count
    smooth_y, smooth_x = zeros, zeros
    for back in range(steps - 1, -1, -1):
        prior_y, prior_x = smooth_y, smooth_x
        near = near_refs[back][...]
        grad_y = 0.5 * (pltpu.roll(near, 7, 0) - pltpu.roll(near, 1, 0))
        grad_x = 0.5 * (pltpu.roll(near, LANES - 1, 1) - pltpu.roll(near, 1, 1))
        corr = near + spread(prior_y) * grad_y + spread(prior_x) * grad_x
        size = jnp.abs(corr)
        below, above = pltpu.roll(corr, 7, 0), pltpu.roll(corr, 1, 0)
        right, left = pltpu.roll(corr, LANES - 1, 1), pltpu.roll(corr, 1, 1)
        flow_y = (below - above) / (jnp.abs(below) + size + jnp.abs(above) + 1.0)
        flow_x = (right - left) / (jnp.abs(right) + size + jnp.abs(left) + 1.0)

        def picked(flow):
            values = []
            for p in range(count):
                here = jnp.logical_and(row == 2, lane == 8 * p + 2)
                spot = jnp.where(here, flow, 0.0)
                values.append(jnp.sum(jnp.sum(spot, axis=1, keepdims=True), axis=0, keepdims=True))
            smooth = []
            for p in range(count):
                total = 0.5 * values[p]
                if p % GC > 0:
                    total = total + 0.25 * values[p - 1]
                if p % GC < GC - 1:
                    total = total + 0.25 * values[p + 1]
                smooth.append(jnp.where(section - back > 0, total, 0.0))
            return smooth

        smooth_y, smooth_x = picked(flow_y), picked(flow_x)

    def laid(values_y, values_x, shape, first):
        out_row = lax.broadcasted_iota(jnp.int32, shape, 0)
        out_lane = lax.broadcasted_iota(jnp.int32, shape, 1)
        tile = jnp.zeros(shape, F32)
        for p in range(count):
            pair = jnp.where(out_row == 0, values_y[p], values_x[p])
            here = jnp.logical_and(out_lane == first + p, out_row < 2)
            tile = jnp.where(here, pair, tile)
        return tile

    smooth_ref[...] = laid(smooth_y, smooth_x, smooth_ref.shape, strip * count)
    prior_ref[...] = laid(prior_y, prior_x, prior_ref.shape, 0)


def map_kernel(corr_ref, prior_ref, out_ref):
    count, edge, _ = corr_ref.shape
    for p in range(count):
        corr = corr_ref[p]
        smooth_y = prior_ref[0:1, p : p + 1]
        smooth_x = prior_ref[1:2, p : p + 1]
        grad_y = jnp.roll(corr, -1, axis=0) - jnp.roll(corr, 1, axis=0)
        grad_x = jnp.roll(corr, -1, axis=1) - jnp.roll(corr, 1, axis=1)
        total = corr + (0.5 * smooth_y) * grad_y + (0.5 * smooth_x) * grad_x
        out_ref[p] = total * (1.0 / edge)


def gradient_matrix(size, edge, up):
    row = lax.broadcasted_iota(jnp.int32, (size, size), 0)
    col = lax.broadcasted_iota(jnp.int32, (size, size), 1)
    out, source = (row, col) if up else (col, row)
    following = jnp.where(out == edge - 1, 0, out + 1)
    before = jnp.where(out == 0, edge - 1, out - 1)
    inside = out < edge
    plus = jnp.where(jnp.logical_and(inside, source == following), 0.5, 0.0)
    minus = jnp.where(jnp.logical_and(inside, source == before), 0.5, 0.0)
    return (plus - minus).astype(BF16)


def render_kernel(count, edge, strips_of, n_block, n_smooth, *refs):
    blocks, smooths = refs[:n_block], refs[n_block : n_block + n_smooth]
    out_ref, onehot, stacked = refs[n_block + n_smooth :]
    rows = count * edge
    part = rows // 4
    rest = edge - LANES
    wide = round_up(rows, LANES)
    me = lax.axis_index("strip")
    smooth = smooths[0][...]
    for other in smooths[1:]:
        smooth = smooth + other[...]
    lanes_all = smooth.shape[1]
    along_y = gradient_matrix(edge, edge, True)
    along_x = gradient_matrix(2 * LANES, edge, False)
    lane = lax.broadcasted_iota(jnp.int32, (part, LANES), 1)
    ones_lane = jnp.where(lane == rest, 1.0, 0.0)
    land = lax.broadcasted_iota(jnp.int32, (rows, LANES), 0).astype(F32)
    first_row = (me * rows).astype(F32)

    def place(message, strip, slot):
        mine = pltpu.roll(smooth, lanes_all - strip * count, 1)
        side = message[rows : rows + part, :].astype(F32)
        for p in range(count):
            halves = []
            for g in (2 * p, 2 * p + 1):
                left = message[g * part : (g + 1) * part, :].astype(F32)
                turned = pltpu.roll(side, (LANES - g * rest) % LANES, 1) if g else side
                halves.append(
                    jnp.concatenate([left, jnp.where(lane < rest, turned, ones_lane)], axis=1)
                )
            base = jnp.concatenate(halves, axis=0)
            base_low = base.astype(BF16)
            grad_y = product(along_y, base_low)
            grad_x = product(base_low, along_x)
            smooth_y, smooth_x = mine[0:1, p : p + 1], mine[1:2, p : p + 1]
            aligned = base + smooth_y * grad_y + smooth_x * grad_x
            stacked[slot * wide + p * edge : slot * wide + (p + 1) * edge, :] = aligned.astype(BF16)
        if wide > rows:
            stacked[slot * wide + rows : (slot + 1) * wide, :] = jnp.zeros(
                (wide - rows, 2 * LANES), BF16
            )
        tail = message[rows + part :, :].astype(F32)
        key = tail[0:8] * 256.0 + tail[8:16] - first_row
        for j in range(wide // LANES):
            onehot[:, slot * wide + j * LANES : slot * wide + (j + 1) * LANES] = jnp.where(
                land == key[j : j + 1, :], 1.0, 0.0
            ).astype(BF16)

    if len(blocks[0].shape) == 2:
        for slot, (block, offset) in enumerate(zip(blocks, strips_of)):
            place(block, jnp.bitwise_xor(me, offset), slot)
        total = product(onehot[...], stacked[...])
    else:

        def step(i, total):
            place(blocks[0].at[i], i, 0)
            return total + product(onehot[...], stacked[...])

        total = lax.fori_loop(0, blocks[0].shape[0], step, jnp.zeros((rows, 2 * LANES), F32))
    counts = jnp.maximum(total[:, edge : edge + 1], 1.0)
    out_ref[...] = (total[:, :edge] / counts).astype(BF16)


def turned(block, axis, distance):
    size = lax.axis_size(axis)
    return lax.ppermute(block, axis, [(i, (i + distance) % size) for i in range(size)])


def swapped(block, offset):
    return lax.ppermute(
        block, "strip", [(i, i ^ offset) for i in range(lax.axis_size("strip"))]
    )


def on_device(image, peaks, row_source, row_weight, col_source, col_weight, owner, render_row):
    pixels = image[0]
    count, edge, _ = pixels.shape
    rows = count * edge
    sections, strips = lax.axis_size("sec"), lax.axis_size("strip")
    dft_cos, dft_sin = dft_tables(edge)
    length = message_rows(rows)
    wide = round_up(rows, LANES)

    message = call(
        base_kernel,
        jax.ShapeDtypeStruct((length, LANES), BF16),
        7,
        scratch=[pltpu.VMEM((16, wide), F32)],
    )(
        pixels,
        row_source[0],
        row_weight[0],
        col_source[0],
        col_weight[0],
        owner[0].reshape(1, rows),
        render_row,
    )
    prior_message = turned(message, "sec", 1)
    table = jax.ShapeDtypeStruct((count, edge, edge), F32)
    img_re, img_im = call(spectrum_kernel, (table, table), 3)(pixels, dft_cos, dft_sin)
    corr, near = call(
        surface_kernel,
        (table, jax.ShapeDtypeStruct((8, LANES), F32)),
        6,
        smem=(5,),
        scratch=[pltpu.VMEM((count, edge + 8, edge), F32)],
    )(prior_message, img_re, img_im, dft_cos, dft_sin, peaks[0])

    few = strips <= 8 and strips & (strips - 1) == 0
    if few:
        offsets = [2 * k for k in range(strips // 2)]
        blocks = [message] + [swapped(message, offset) for offset in offsets[1:]]
        blocks = blocks + [swapped(block, 1) for block in blocks]
        offsets = offsets + [offset + 1 for offset in offsets]
    else:
        blocks, offsets = [lax.all_gather(message, "strip")], None

    nears = [near] + [turned(near, "sec", k) for k in range(1, sections - 1)]
    patches_all = round_up(count * strips, LANES)
    smooth, prior = call(
        functools.partial(chain_kernel, count, len(nears)),
        (
            jax.ShapeDtypeStruct((8, patches_all), F32),
            jax.ShapeDtypeStruct((8, LANES), F32),
        ),
        len(nears),
    )(*nears)
    corr_map = call(map_kernel, table, 2)(corr, prior)
    if few:
        total = smooth
        for offset in offsets[1 : strips // 2]:
            total = total + swapped(smooth, offset)
        smooths = [total, swapped(total, 1)]
    else:
        smooths = [lax.psum(smooth, "strip")]
    slots = len(blocks)
    render = call(
        functools.partial(render_kernel, count, edge, offsets, len(blocks), len(smooths)),
        jax.ShapeDtypeStruct((rows, edge), BF16),
        len(blocks) + len(smooths),
        scratch=[
            pltpu.VMEM((rows, slots * wide), BF16),
            pltpu.VMEM((slots * wide, 2 * LANES), BF16),
        ],
    )(*blocks, *smooths)
    return (render[None], corr_map[None])


def solution(mesh):
    placed = (
        P("sec", "strip", None, None),
        P("sec", "strip", None),
        P("sec", "strip", None),
        P("sec", "strip", None),
        P("sec", "strip", None),
        P("sec", "strip", None),
        P("sec", "strip", None),
        P("sec", "strip"),
    )
    return jax.shard_map(
        on_device,
        mesh=mesh,
        in_specs=placed,
        out_specs=(P("sec", "strip", None), P("sec", "strip", None, None)),
        check_vma=False,
    )
```

```python
import functools

import jax
import jax.numpy as jnp
import numpy as np
from jax import lax
from jax.experimental import pallas as pl
from jax.experimental.pallas import tpu as pltpu
from jax.sharding import PartitionSpec as P

GC = 2
LANES = 128
TWO_PI = 2.0 * 3.141592653589793
F32 = jnp.float32
BF16 = jnp.bfloat16
VMEM_BYTES = 16 * 1024 * 1024


def product(left, right):
    return jnp.dot(left, right, preferred_element_type=F32)


def dft_tables(edge):
    positions = np.arange(edge, dtype=np.int32)
    phases = positions[:, None] * positions[None, :] % edge
    angles = phases.astype(np.float32) * np.float32(TWO_PI / edge)
    return jnp.asarray(np.cos(angles), BF16), jnp.asarray(np.sin(angles), BF16)


def round_up(size, unit):
    return -(-size // unit) * unit


def message_rows(rows):
    return rows + rows // 4 + 16


def call(kernel, out_shape, n_in, space=pltpu.VMEM, scratch=(), vmem=VMEM_BYTES, flops=1000000000):
    specs = [pl.BlockSpec(memory_space=space) for _ in range(n_in)]
    outs = jax.tree.map(lambda _: pl.BlockSpec(memory_space=pltpu.VMEM), out_shape)
    return pl.pallas_call(
        kernel,
        out_shape=out_shape,
        in_specs=specs,
        out_specs=outs,
        scratch_shapes=list(scratch),
        compiler_params=pltpu.CompilerParams(vmem_limit_bytes=vmem),
        cost_estimate=pl.CostEstimate(flops=flops, bytes_accessed=500000, transcendentals=0),
    )


def warp_matrix_t(source, weight, edge):
    spots = lax.broadcasted_iota(jnp.int32, (edge, edge), 0)
    following = jnp.where(source == edge - 1, 0, source + 1)
    first = jnp.where(spots == source, weight, 0.0)
    second = jnp.where(spots == following, 1.0 - weight, 0.0)
    return (first + second).astype(BF16)


def base_kernel(*refs):
    sources, out_ref, targets, (keys, sems) = refs[:7], refs[7], refs[8:15], refs[15:]
    copies = [
        pltpu.make_async_copy(source, target, sems.at[i])
        for i, (source, target) in enumerate(zip(sources, targets))
    ]
    for copy in copies:
        copy.start()
    image_ref, row_src, row_wt, col_src, col_wt, owner_ref, target_ref = targets
    for copy in copies[1:]:
        copy.wait()
    count, edge, _ = image_ref.shape
    rows = count * edge
    part = rows // 4
    keys[...] = jnp.full(keys.shape, -1.0, F32)
    row_ts, col_ts = [], []
    for p in range(count):
        row_ts.append(warp_matrix_t(row_src[p : p + 1, :], row_wt[p : p + 1, :], edge))
        col_ts.append(warp_matrix_t(col_src[p : p + 1, :], col_wt[p : p + 1, :], edge))
    key = owner_ref[...] * rows + target_ref[...]
    keys[0:1, 0:rows] = (key >> 8).astype(F32)
    keys[8:9, 0:rows] = (key & 255).astype(F32)
    wide = keys.shape[1] // LANES
    blank = jnp.full((8 - wide, LANES), -1.0, F32)
    lines = []
    for half in (0, 8):
        lines += [keys[half : half + 1, j * LANES : (j + 1) * LANES] for j in range(wide)]
        lines += [blank]
    out_ref[rows + part :, :] = jnp.concatenate(lines, axis=0).astype(BF16)
    copies[0].wait()
    pieces = []
    for p in range(count):
        row_warped = lax.dot_general(
            row_ts[p], image_ref[p], (((0,), (0,)), ((), ())), preferred_element_type=F32
        ).astype(BF16)
        base = product(row_warped, col_ts[p])
        out_ref[p * edge : (p + 1) * edge, :] = base[:, :LANES].astype(BF16)
        right = base[:, LANES:]
        pieces += [right[:part], right[part:]]
    out_ref[rows : rows + part, :] = jnp.concatenate(pieces, axis=1).astype(BF16)


def spectrum_of(pixels, dft_cos, dft_sin, count, edge):
    half_re = product(pixels, dft_cos).astype(BF16)
    half_im = (-product(pixels, dft_sin)).astype(BF16)
    spectra = []
    for p in range(count):
        h_re = half_re[p * edge : (p + 1) * edge]
        h_im = half_im[p * edge : (p + 1) * edge]
        spectra.append(
            (
                product(dft_cos, h_re) + product(dft_sin, h_im),
                product(dft_cos, h_im) - product(dft_sin, h_re),
            )
        )
    return spectra


def spectrum_kernel(
    image_ref,
    cos_ref,
    sin_ref,
    peaks_ref,
    message_ref,
    re_ref,
    im_ref,
    cos_row,
    sin_row,
    cos_col,
    sin_col,
    copied_ref,
):
    count, edge, _ = image_ref.shape
    copied_ref[...] = message_ref[...]
    dft_cos, dft_sin = cos_ref[...], sin_ref[...]
    pixels = image_ref[...].reshape(count * edge, edge)
    spectra = spectrum_of(pixels, dft_cos, dft_sin, count, edge)
    for p, (s_re, s_im) in enumerate(spectra):
        re_ref[p] = s_re
        im_ref[p] = s_im

    def wrap(spot):
        return jnp.where(spot < 0, spot + edge, jnp.where(spot >= edge, spot - edge, spot))

    row = lax.broadcasted_iota(jnp.int32, (16, edge), 0)
    row_lane = lax.broadcasted_iota(jnp.int32, (16, edge), 1)
    col = lax.broadcasted_iota(jnp.int32, (edge, LANES), 0)
    col_lane = lax.broadcasted_iota(jnp.int32, (edge, LANES), 1)
    for p in range(count):
        spot = wrap(peaks_ref[p : p + 1, 0:1] + (row - 2))
        pick = jnp.where(jnp.logical_and(row < 5, row_lane == spot), 1.0, 0.0).astype(BF16)
        cos_row[p] = product(pick, dft_cos).astype(BF16)
        sin_row[p] = product(pick, dft_sin).astype(BF16)
        step = col_lane - (8 * p + 2)
        spot = wrap(peaks_ref[p : p + 1, 1:2] + step)
        near = jnp.logical_and(step >= -2, step <= 2)
        pick = jnp.where(jnp.logical_and(near, col == spot), 1.0, 0.0).astype(BF16)
        cos_col[p] = product(dft_cos, pick).astype(BF16)
        sin_col[p] = product(dft_sin, pick).astype(BF16)


def near_kernel(
    message_ref,
    im_re_ref,
    im_im_ref,
    cos_ref,
    sin_ref,
    cos_row,
    sin_row,
    cos_col,
    sin_col,
    near_ref,
    cross_re_ref,
    cross_im_ref,
):
    count, edge, _ = im_re_ref.shape
    rows = count * edge
    part = rows // 4
    rest = edge - LANES
    dft_cos, dft_sin = cos_ref[...], sin_ref[...]
    side = message_ref[rows : rows + part, :].astype(F32)
    groups = []
    for g in range(4):
        left = message_ref[g * part : (g + 1) * part, :].astype(F32)
        groups.append(jnp.concatenate([left, side[:, g * rest : (g + 1) * rest]], axis=1))
    pixels = jnp.concatenate(groups, axis=0)
    pixels = jnp.where(lax.axis_index("sec") > 0, pixels, 0.0).astype(BF16)
    spectra = spectrum_of(pixels, dft_cos, dft_sin, count, edge)
    total = None
    for p, (ref_re, ref_im) in enumerate(spectra):
        img_re, img_im = im_re_ref[p], im_im_ref[p]
        cross_re = (ref_re * img_re + ref_im * img_im).astype(BF16)
        cross_im = (ref_im * img_re - ref_re * img_im).astype(BF16)
        cross_re_ref[p] = cross_re
        cross_im_ref[p] = cross_im
        back_re = (product(cross_re, cos_col[p]) - product(cross_im, sin_col[p])).astype(BF16)
        back_im = (product(cross_re, sin_col[p]) + product(cross_im, cos_col[p])).astype(BF16)
        near = product(cos_row[p], back_re) - product(sin_row[p], back_im)
        total = near if total is None else total + near
    near_ref[...] = total[0:8] * (1.0 / (edge * edge))


def chain_kernel(count, steps, *refs):
    near_refs, (smooth_ref, prior_ref) = refs[:steps], refs[-2:]
    section = lax.axis_index("sec")
    strip = lax.axis_index("strip")
    row = lax.broadcasted_iota(jnp.int32, (8, LANES), 0)
    lane = lax.broadcasted_iota(jnp.int32, (8, LANES), 1)

    def spread(values):
        tile = jnp.broadcast_to(values[0], (8, LANES))
        for p in range(1, count):
            tile = jnp.where(lane >= 8 * p, values[p], tile)
        return tile

    zeros = [jnp.zeros((1, 1), F32)] * count
    smooth_y, smooth_x = zeros, zeros
    for back in range(steps - 1, -1, -1):
        prior_y, prior_x = smooth_y, smooth_x
        near = near_refs[back][...]
        grad_y = 0.5 * (pltpu.roll(near, 7, 0) - pltpu.roll(near, 1, 0))
        grad_x = 0.5 * (pltpu.roll(near, LANES - 1, 1) - pltpu.roll(near, 1, 1))
        corr = near + spread(prior_y) * grad_y + spread(prior_x) * grad_x
        size = jnp.abs(corr)
        below, above = pltpu.roll(corr, 7, 0), pltpu.roll(corr, 1, 0)
        right, left = pltpu.roll(corr, LANES - 1, 1), pltpu.roll(corr, 1, 1)
        flow_y = (below - above) / (jnp.abs(below) + size + jnp.abs(above) + 1.0)
        flow_x = (right - left) / (jnp.abs(right) + size + jnp.abs(left) + 1.0)

        def picked(flow):
            values = []
            for p in range(count):
                here = jnp.logical_and(row == 2, lane == 8 * p + 2)
                spot = jnp.where(here, flow, 0.0)
                values.append(jnp.sum(jnp.sum(spot, axis=1, keepdims=True), axis=0, keepdims=True))
            smooth = []
            for p in range(count):
                total = 0.5 * values[p]
                if p % GC > 0:
                    total = total + 0.25 * values[p - 1]
                if p % GC < GC - 1:
                    total = total + 0.25 * values[p + 1]
                smooth.append(jnp.where(section - back > 0, total, 0.0))
            return smooth

        smooth_y, smooth_x = picked(flow_y), picked(flow_x)

    def laid(values_y, values_x, shape, first):
        out_row = lax.broadcasted_iota(jnp.int32, shape, 0)
        out_lane = lax.broadcasted_iota(jnp.int32, shape, 1)
        tile = jnp.zeros(shape, F32)
        for p in range(count):
            pair = jnp.where(out_row == 0, values_y[p], values_x[p])
            here = jnp.logical_and(out_lane == first + p, out_row < 2)
            tile = jnp.where(here, pair, tile)
        return tile

    smooth_ref[...] = laid(smooth_y, smooth_x, smooth_ref.shape, strip * count)
    prior_ref[...] = laid(prior_y, prior_x, prior_ref.shape, 0)


def surface_kernel(cross_re_ref, cross_im_ref, cos_ref, sin_ref, corr_ref, grad_y_ref, grad_x_ref):
    count, edge, _ = cross_re_ref.shape
    dft_cos, dft_sin = cos_ref[...], sin_ref[...]
    for p in range(count):
        cross_re, cross_im = cross_re_ref[p], cross_im_ref[p]
        back_re = (product(cross_re, dft_cos) - product(cross_im, dft_sin)).astype(BF16)
        back_im = (product(cross_re, dft_sin) + product(cross_im, dft_cos)).astype(BF16)
        corr = product(dft_cos, back_re) - product(dft_sin, back_im)
        corr = corr * (1.0 / (edge * edge * edge))
        corr_ref[p] = corr
        grad_y_ref[p] = 0.5 * (jnp.roll(corr, -1, axis=0) - jnp.roll(corr, 1, axis=0))
        grad_x_ref[p] = 0.5 * (jnp.roll(corr, -1, axis=1) - jnp.roll(corr, 1, axis=1))


def map_kernel(corr_ref, grad_y_ref, grad_x_ref, prior_ref, smooth_ref, out_ref, passed_ref):
    passed_ref[...] = smooth_ref[...]
    for p in range(corr_ref.shape[0]):
        smooth_y = prior_ref[0:1, p : p + 1]
        smooth_x = prior_ref[1:2, p : p + 1]
        out_ref[p] = corr_ref[p] + smooth_y * grad_y_ref[p] + smooth_x * grad_x_ref[p]


def gradient_matrix(size, edge, up):
    row = lax.broadcasted_iota(jnp.int32, (size, size), 0)
    col = lax.broadcasted_iota(jnp.int32, (size, size), 1)
    out, source = (row, col) if up else (col, row)
    following = jnp.where(out == edge - 1, 0, out + 1)
    before = jnp.where(out == 0, edge - 1, out - 1)
    inside = out < edge
    plus = jnp.where(jnp.logical_and(inside, source == following), 0.5, 0.0)
    minus = jnp.where(jnp.logical_and(inside, source == before), 0.5, 0.0)
    return (plus - minus).astype(BF16)


def lay_out(messages, count, edge, keys, onehot, base_out, grad_y_out, grad_x_out):
    rows = count * edge
    part = rows // 4
    rest = edge - LANES
    deep = onehot.shape[1]
    used = len(messages) * rows
    along_y = gradient_matrix(edge, edge, True)
    along_x = gradient_matrix(2 * LANES, edge, False)
    lane = lax.broadcasted_iota(jnp.int32, (part, LANES), 1)
    ones_lane = jnp.where(lane == rest, 1.0, 0.0)
    land = lax.broadcasted_iota(jnp.int32, (rows, LANES), 0).astype(F32)
    first_row = (lax.axis_index("strip") * rows).astype(F32)
    if deep > used:
        keys[...] = jnp.full(keys.shape, -1.0, F32)
        base_out[used:, :] = jnp.zeros((deep - used, 2 * LANES), BF16)
    for slot, message in enumerate(messages):
        side = message[rows : rows + part, :].astype(F32)
        for p in range(count):
            halves = []
            for g in (2 * p, 2 * p + 1):
                left = message[g * part : (g + 1) * part, :].astype(F32)
                turned_side = pltpu.roll(side, (LANES - g * rest) % LANES, 1) if g else side
                halves.append(
                    jnp.concatenate([left, jnp.where(lane < rest, turned_side, ones_lane)], axis=1)
                )
            base = jnp.concatenate(halves, axis=0).astype(BF16)
            place = slice(slot * rows + p * edge, slot * rows + (p + 1) * edge)
            base_out[place, :] = base
            grad_y_out[place, :] = product(along_y, base).astype(BF16)
            grad_x_out[place, :] = product(base, along_x).astype(BF16)
        tail = message[rows + part :, :].astype(F32)
        key = tail[0:8] * 256.0 + tail[8:16] - first_row
        for j in range(0, rows, LANES):
            size = min(LANES, rows - j)
            line = key[j // LANES : j // LANES + 1, :size]
            keys[0:1, slot * rows + j : slot * rows + j + size] = line
    for j in range(0, deep, LANES):
        hit = land == keys[0:1, j : j + LANES]
        onehot[:, j : j + LANES] = jnp.where(hit, 1.0, 0.0).astype(BF16)


def align_rows(smooth, strip, count, edge, slot, base_in, grad_y_in, grad_x_in, stacked):
    mine = pltpu.roll(smooth, smooth.shape[1] - strip * count, 1)
    for p in range(count):
        place = slice(slot * count * edge + p * edge, slot * count * edge + (p + 1) * edge)
        smooth_y = jnp.broadcast_to(mine[0:1, p : p + 1], (edge, 2 * LANES)).astype(BF16)
        smooth_x = jnp.broadcast_to(mine[1:2, p : p + 1], (edge, 2 * LANES)).astype(BF16)
        change = smooth_y * grad_y_in[place, :] + smooth_x * grad_x_in[place, :]
        stacked[place, :] = base_in[place, :] + change


def averaged(total, edge):
    sums = jnp.transpose(total)
    return (sums[:edge] / jnp.maximum(sums[edge : edge + 1], 1.0)).astype(BF16)


def prepare_kernel(count, edge, slots, *refs):
    lay_out(refs[:slots], count, edge, refs[-1], *refs[-5:-1])


def render_kernel(count, edge, groups, *refs):
    prepared = refs[: 4 * len(groups)]
    smooth_a, smooth_b, out_ref = refs[4 * len(groups) : 4 * len(groups) + 3]
    stacks = refs[4 * len(groups) + 3 :]
    me = lax.axis_index("strip")
    smooth = smooth_a[...] + smooth_b[...]
    total = None
    for i, offsets in enumerate(groups):
        onehot, base, grad_y, grad_x = prepared[4 * i : 4 * i + 4]
        for slot, offset in enumerate(offsets):
            strip = jnp.bitwise_xor(me, offset)
            align_rows(smooth, strip, count, edge, slot, base, grad_y, grad_x, stacks[i])
        used = len(offsets) * count * edge
        if stacks[i].shape[0] > used:
            stacks[i][used:, :] = base[used:, :]
        part = product(onehot[...], stacks[i][...])
        total = part if total is None else total + part
    out_ref[...] = averaged(total, edge)


def render_all_kernel(
    count, edge, messages, smooth_ref, out_ref, onehot, base, grad_y, grad_x, keys, stacked
):
    rows = count * edge

    def step(i, total):
        lay_out([messages.at[i]], count, edge, keys, onehot, base, grad_y, grad_x)
        align_rows(smooth_ref[...], i, count, edge, 0, base, grad_y, grad_x, stacked)
        if stacked.shape[0] > rows:
            stacked[rows:, :] = base[rows:, :]
        return total + product(onehot[...], stacked[...])

    total = lax.fori_loop(0, messages.shape[0], step, jnp.zeros((rows, 2 * LANES), F32))
    out_ref[...] = averaged(total, edge)


def turned(block, axis, distance):
    size = lax.axis_size(axis)
    return lax.ppermute(block, axis, [(i, (i + distance) % size) for i in range(size)])


def swapped(block, offset):
    return lax.ppermute(
        block, "strip", [(i, i ^ offset) for i in range(lax.axis_size("strip"))]
    )


def on_device(image, peaks, row_source, row_weight, col_source, col_weight, owner, render_row):
    pixels = image[0]
    count, edge, _ = pixels.shape
    rows = count * edge
    sections, strips = lax.axis_size("sec"), lax.axis_size("strip")
    dft_cos, dft_sin = dft_tables(edge)
    length = message_rows(rows)
    wide = round_up(rows, LANES)

    inputs = (
        pixels,
        row_source[0],
        row_weight[0],
        col_source[0],
        col_weight[0],
        owner[0].reshape(1, rows),
        render_row,
    )
    message = call(
        base_kernel,
        jax.ShapeDtypeStruct((length, LANES), BF16),
        len(inputs),
        space=pltpu.HBM,
        scratch=[pltpu.VMEM(x.shape, x.dtype) for x in inputs]
        + [pltpu.VMEM((16, wide), F32), pltpu.SemaphoreType.DMA((len(inputs),))],
    )(*[pltpu.with_memory_space_constraint(x, pltpu.HBM) for x in inputs])
    prior_message = turned(message, "sec", 1)

    def table(*shape, kind=BF16):
        return jax.ShapeDtypeStruct(shape, kind)

    square = table(count, edge, edge, kind=F32)
    slim, tall = table(count, 16, edge), table(count, edge, LANES)
    *spectra, copied = call(
        spectrum_kernel,
        (square, square, slim, slim, tall, tall, table(length, LANES)),
        5,
    )(pixels, dft_cos, dft_sin, peaks[0], message)
    near, cross_re, cross_im = call(
        near_kernel,
        (table(8, LANES, kind=F32), table(count, edge, edge), table(count, edge, edge)),
        9,
    )(prior_message, *spectra[:2], dft_cos, dft_sin, *spectra[2:])

    surfaces = call(surface_kernel, (square,) * 3, 4)(cross_re, cross_im, dft_cos, dft_sin)

    def laid(slots):
        deep = round_up(slots * rows, LANES)
        return (table(rows, deep),) + (table(deep, 2 * LANES),) * 3

    def key_line(slots):
        return pltpu.VMEM((8, round_up(slots * rows, LANES)), F32)

    def stack(slots):
        return pltpu.VMEM((round_up(slots * rows, LANES), 2 * LANES), BF16)

    few = strips <= 8 and strips & (strips - 1) == 0
    order = [surfaces[0]]
    if few:
        offsets = [2 * k for k in range(strips // 2)]
        blocks = [copied] + [swapped(copied, offset) for offset in offsets[1:]]

        def prepared(group, after):
            return call(
                functools.partial(prepare_kernel, count, edge, len(group)),
                laid(len(group)),
                len(group) + 1,
                scratch=[key_line(len(group))],
            )(*group, after)

        early_side = prepared([copied, swapped(message, 1)], near)
        order.append(early_side[0])

    nears = [near] + [turned(near, "sec", k) for k in range(1, sections - 1)]
    patches_all = round_up(count * strips, LANES)
    smooth, prior = call(
        functools.partial(chain_kernel, count, len(nears)),
        (table(8, patches_all, kind=F32), table(8, LANES, kind=F32)),
        len(nears) + len(order),
    )(*nears, *order)
    corr_map, passed = call(map_kernel, (square, table(8, patches_all, kind=F32)), 5)(
        *surfaces, prior, smooth
    )

    rendered = table(edge, rows)
    if few:
        total = sum([swapped(smooth, offset) for offset in offsets[1:]], passed)
        late_side = prepared(blocks[1:] + [swapped(block, 1) for block in blocks[1:]], total)
        groups = [0, 1], offsets[1:] + [offset + 1 for offset in offsets[1:]]
        render = call(
            functools.partial(render_kernel, count, edge, groups),
            rendered,
            10,
            scratch=[stack(len(group)) for group in groups],
        )(*early_side, *late_side, total, swapped(total, 1))
    else:
        render = call(
            functools.partial(render_all_kernel, count, edge),
            rendered,
            2,
            scratch=[pltpu.VMEM(x.shape, x.dtype) for x in laid(1)] + [key_line(1), stack(1)],
            vmem=2 * strips * length * LANES * 2 + VMEM_BYTES,
        )(lax.all_gather(copied, "strip"), lax.psum(passed, "strip"))
    return (render.T[None], corr_map[None])


def solution(mesh):
    placed = (
        P("sec", "strip", None, None),
        P("sec", "strip", None),
        P("sec", "strip", None),
        P("sec", "strip", None),
        P("sec", "strip", None),
        P("sec", "strip", None),
        P("sec", "strip", None),
        P("sec", "strip"),
    )
    return jax.shard_map(
        on_device,
        mesh=mesh,
        in_specs=placed,
        out_specs=(P("sec", "strip", None), P("sec", "strip", None, None)),
        check_vma=False,
    )
```

```python
import functools

import jax
import jax.numpy as jnp
import numpy as np
from jax import lax
from jax.experimental import pallas as pl
from jax.experimental.pallas import tpu as pltpu
from jax.sharding import PartitionSpec as P

GC = 2
LANES = 128
TWO_PI = 2.0 * 3.141592653589793
F32 = jnp.float32
BF16 = jnp.bfloat16
VMEM_BYTES = 16 * 1024 * 1024


def product(left, right):
    return jnp.dot(left, right, preferred_element_type=F32)


def dft_tables(edge):
    positions = np.arange(edge, dtype=np.int32)
    phases = positions[:, None] * positions[None, :] % edge
    angles = phases.astype(np.float32) * np.float32(TWO_PI / edge)
    return jnp.asarray(np.cos(angles), BF16), jnp.asarray(np.sin(angles), BF16)


def round_up(size, unit):
    return -(-size // unit) * unit


def message_rows(rows):
    return rows + rows // 4 + 16


def call(kernel, out_shape, n_in, space=pltpu.VMEM, scratch=(), vmem=VMEM_BYTES, flops=1000000000):
    specs = [pl.BlockSpec(memory_space=space) for _ in range(n_in)]
    outs = jax.tree.map(lambda _: pl.BlockSpec(memory_space=pltpu.VMEM), out_shape)
    return pl.pallas_call(
        kernel,
        out_shape=out_shape,
        in_specs=specs,
        out_specs=outs,
        scratch_shapes=list(scratch),
        compiler_params=pltpu.CompilerParams(vmem_limit_bytes=vmem),
        cost_estimate=pl.CostEstimate(flops=flops, bytes_accessed=500000, transcendentals=0),
    )


def warp_matrix_t(source, weight, edge):
    spots = lax.broadcasted_iota(jnp.int32, (edge, edge), 0)
    following = jnp.where(source == edge - 1, 0, source + 1)
    first = jnp.where(spots == source, weight, 0.0)
    second = jnp.where(spots == following, 1.0 - weight, 0.0)
    return (first + second).astype(BF16)


def base_kernel(*refs):
    sources, out_ref, targets, (keys, sems) = refs[:7], refs[7], refs[8:15], refs[15:]
    copies = [
        pltpu.make_async_copy(source, target, sems.at[i])
        for i, (source, target) in enumerate(zip(sources, targets))
    ]
    for copy in copies:
        copy.start()
    image_ref, row_src, row_wt, col_src, col_wt, owner_ref, target_ref = targets
    for copy in copies[1:]:
        copy.wait()
    count, edge, _ = image_ref.shape
    rows = count * edge
    part = rows // 4
    keys[...] = jnp.full(keys.shape, -1.0, F32)
    row_ts, col_ts = [], []
    for p in range(count):
        row_ts.append(warp_matrix_t(row_src[p : p + 1, :], row_wt[p : p + 1, :], edge))
        col_ts.append(warp_matrix_t(col_src[p : p + 1, :], col_wt[p : p + 1, :], edge))
    key = owner_ref[...] * rows + target_ref[...]
    keys[0:1, 0:rows] = (key >> 8).astype(F32)
    keys[8:9, 0:rows] = (key & 255).astype(F32)
    wide = keys.shape[1] // LANES
    blank = jnp.full((8 - wide, LANES), -1.0, F32)
    lines = []
    for half in (0, 8):
        lines += [keys[half : half + 1, j * LANES : (j + 1) * LANES] for j in range(wide)]
        lines += [blank]
    out_ref[rows + part :, :] = jnp.concatenate(lines, axis=0).astype(BF16)
    copies[0].wait()
    pieces = []
    for p in range(count):
        row_warped = lax.dot_general(
            row_ts[p], image_ref[p], (((0,), (0,)), ((), ())), preferred_element_type=F32
        ).astype(BF16)
        base = product(row_warped, col_ts[p])
        out_ref[p * edge : (p + 1) * edge, :] = base[:, :LANES].astype(BF16)
        right = base[:, LANES:]
        pieces += [right[:part], right[part:]]
    out_ref[rows : rows + part, :] = jnp.concatenate(pieces, axis=1).astype(BF16)


def spectrum_of(pixels, dft_cos, dft_sin, count, edge):
    half_re = product(pixels, dft_cos).astype(BF16)
    half_im = (-product(pixels, dft_sin)).astype(BF16)
    spectra = []
    for p in range(count):
        h_re = half_re[p * edge : (p + 1) * edge]
        h_im = half_im[p * edge : (p + 1) * edge]
        spectra.append(
            (
                product(dft_cos, h_re) + product(dft_sin, h_im),
                product(dft_cos, h_im) - product(dft_sin, h_re),
            )
        )
    return spectra


def spectrum_kernel(
    image_ref,
    cos_ref,
    sin_ref,
    peaks_ref,
    message_ref,
    re_ref,
    im_ref,
    cos_row,
    sin_row,
    cos_col,
    sin_col,
    copied_ref,
):
    count, edge, _ = image_ref.shape
    copied_ref[...] = message_ref[...]
    dft_cos, dft_sin = cos_ref[...], sin_ref[...]
    pixels = image_ref[...].reshape(count * edge, edge)
    spectra = spectrum_of(pixels, dft_cos, dft_sin, count, edge)
    for p, (s_re, s_im) in enumerate(spectra):
        re_ref[p] = s_re
        im_ref[p] = s_im

    def wrap(spot):
        return jnp.where(spot < 0, spot + edge, jnp.where(spot >= edge, spot - edge, spot))

    row = lax.broadcasted_iota(jnp.int32, (16, edge), 0)
    row_lane = lax.broadcasted_iota(jnp.int32, (16, edge), 1)
    col = lax.broadcasted_iota(jnp.int32, (edge, LANES), 0)
    col_lane = lax.broadcasted_iota(jnp.int32, (edge, LANES), 1)
    for p in range(count):
        spot = wrap(peaks_ref[p : p + 1, 0:1] + (row - 2))
        pick = jnp.where(jnp.logical_and(row < 5, row_lane == spot), 1.0, 0.0).astype(BF16)
        cos_row[p] = product(pick, dft_cos).astype(BF16)
        sin_row[p] = product(pick, dft_sin).astype(BF16)
        step = col_lane - (8 * p + 2)
        spot = wrap(peaks_ref[p : p + 1, 1:2] + step)
        near = jnp.logical_and(step >= -2, step <= 2)
        pick = jnp.where(jnp.logical_and(near, col == spot), 1.0, 0.0).astype(BF16)
        cos_col[p] = product(dft_cos, pick).astype(BF16)
        sin_col[p] = product(dft_sin, pick).astype(BF16)


def near_kernel(
    message_ref,
    im_re_ref,
    im_im_ref,
    cos_ref,
    sin_ref,
    cos_row,
    sin_row,
    cos_col,
    sin_col,
    near_ref,
    cross_re_ref,
    cross_im_ref,
):
    count, edge, _ = im_re_ref.shape
    rows = count * edge
    part = rows // 4
    rest = edge - LANES
    dft_cos, dft_sin = cos_ref[...], sin_ref[...]
    side = message_ref[rows : rows + part, :].astype(F32)
    groups = []
    for g in range(4):
        left = message_ref[g * part : (g + 1) * part, :].astype(F32)
        groups.append(jnp.concatenate([left, side[:, g * rest : (g + 1) * rest]], axis=1))
    pixels = jnp.concatenate(groups, axis=0)
    pixels = jnp.where(lax.axis_index("sec") > 0, pixels, 0.0).astype(BF16)
    spectra = spectrum_of(pixels, dft_cos, dft_sin, count, edge)
    total = None
    for p, (ref_re, ref_im) in enumerate(spectra):
        img_re, img_im = im_re_ref[p], im_im_ref[p]
        cross_re = (ref_re * img_re + ref_im * img_im).astype(BF16)
        cross_im = (ref_im * img_re - ref_re * img_im).astype(BF16)
        cross_re_ref[p] = cross_re
        cross_im_ref[p] = cross_im
        back_re = (product(cross_re, cos_col[p]) - product(cross_im, sin_col[p])).astype(BF16)
        back_im = (product(cross_re, sin_col[p]) + product(cross_im, cos_col[p])).astype(BF16)
        near = product(cos_row[p], back_re) - product(sin_row[p], back_im)
        total = near if total is None else total + near
    near_ref[...] = total[0:8] * (1.0 / (edge * edge))


def chain_kernel(count, steps, *refs):
    near_refs, (smooth_ref, prior_ref) = refs[:steps], refs[-2:]
    section = lax.axis_index("sec")
    strip = lax.axis_index("strip")
    row = lax.broadcasted_iota(jnp.int32, (8, LANES), 0)
    lane = lax.broadcasted_iota(jnp.int32, (8, LANES), 1)

    def spread(values):
        tile = jnp.broadcast_to(values[0], (8, LANES))
        for p in range(1, count):
            tile = jnp.where(lane >= 8 * p, values[p], tile)
        return tile

    zeros = [jnp.zeros((1, 1), F32)] * count
    smooth_y, smooth_x = zeros, zeros
    for back in range(steps - 1, -1, -1):
        prior_y, prior_x = smooth_y, smooth_x
        near = near_refs[back][...]
        grad_y = 0.5 * (pltpu.roll(near, 7, 0) - pltpu.roll(near, 1, 0))
        grad_x = 0.5 * (pltpu.roll(near, LANES - 1, 1) - pltpu.roll(near, 1, 1))
        corr = near + spread(prior_y) * grad_y + spread(prior_x) * grad_x
        size = jnp.abs(corr)
        below, above = pltpu.roll(corr, 7, 0), pltpu.roll(corr, 1, 0)
        right, left = pltpu.roll(corr, LANES - 1, 1), pltpu.roll(corr, 1, 1)
        flow_y = (below - above) / (jnp.abs(below) + size + jnp.abs(above) + 1.0)
        flow_x = (right - left) / (jnp.abs(right) + size + jnp.abs(left) + 1.0)

        def picked(flow):
            values = []
            for p in range(count):
                here = jnp.logical_and(row == 2, lane == 8 * p + 2)
                spot = jnp.where(here, flow, 0.0)
                values.append(jnp.sum(jnp.sum(spot, axis=1, keepdims=True), axis=0, keepdims=True))
            smooth = []
            for p in range(count):
                total = 0.5 * values[p]
                if p % GC > 0:
                    total = total + 0.25 * values[p - 1]
                if p % GC < GC - 1:
                    total = total + 0.25 * values[p + 1]
                smooth.append(jnp.where(section - back > 0, total, 0.0))
            return smooth

        smooth_y, smooth_x = picked(flow_y), picked(flow_x)

    def laid(values_y, values_x, shape, first):
        out_row = lax.broadcasted_iota(jnp.int32, shape, 0)
        out_lane = lax.broadcasted_iota(jnp.int32, shape, 1)
        tile = jnp.zeros(shape, F32)
        for p in range(count):
            pair = jnp.where(out_row == 0, values_y[p], values_x[p])
            here = jnp.logical_and(out_lane == first + p, out_row < 2)
            tile = jnp.where(here, pair, tile)
        return tile

    smooth_ref[...] = laid(smooth_y, smooth_x, smooth_ref.shape, strip * count)
    prior_ref[...] = laid(prior_y, prior_x, prior_ref.shape, 0)


def surface_kernel(cross_re_ref, cross_im_ref, cos_ref, sin_ref, corr_ref, grad_y_ref, grad_x_ref):
    count, edge, _ = cross_re_ref.shape
    dft_cos, dft_sin = cos_ref[...], sin_ref[...]
    for p in range(count):
        cross_re, cross_im = cross_re_ref[p], cross_im_ref[p]
        back_re = (product(cross_re, dft_cos) - product(cross_im, dft_sin)).astype(BF16)
        back_im = (product(cross_re, dft_sin) + product(cross_im, dft_cos)).astype(BF16)
        corr = product(dft_cos, back_re) - product(dft_sin, back_im)
        corr = corr * (1.0 / (edge * edge * edge))
        corr_ref[p] = corr
        grad_y_ref[p] = 0.5 * (jnp.roll(corr, -1, axis=0) - jnp.roll(corr, 1, axis=0))
        grad_x_ref[p] = 0.5 * (jnp.roll(corr, -1, axis=1) - jnp.roll(corr, 1, axis=1))


def map_kernel(corr_ref, grad_y_ref, grad_x_ref, prior_ref, smooth_ref, out_ref, passed_ref):
    passed_ref[...] = smooth_ref[...]
    for p in range(corr_ref.shape[0]):
        smooth_y = prior_ref[0:1, p : p + 1]
        smooth_x = prior_ref[1:2, p : p + 1]
        out_ref[p] = corr_ref[p] + smooth_y * grad_y_ref[p] + smooth_x * grad_x_ref[p]


def gradient_matrix(size, edge, up):
    row = lax.broadcasted_iota(jnp.int32, (size, size), 0)
    col = lax.broadcasted_iota(jnp.int32, (size, size), 1)
    out, source = (row, col) if up else (col, row)
    following = jnp.where(out == edge - 1, 0, out + 1)
    before = jnp.where(out == 0, edge - 1, out - 1)
    inside = out < edge
    plus = jnp.where(jnp.logical_and(inside, source == following), 0.5, 0.0)
    minus = jnp.where(jnp.logical_and(inside, source == before), 0.5, 0.0)
    return (plus - minus).astype(BF16)


def lay_out(messages, count, edge, keys, onehot, base_out, grad_y_out, grad_x_out):
    rows = count * edge
    part = rows // 4
    rest = edge - LANES
    deep = onehot.shape[1]
    used = len(messages) * rows
    along_y = gradient_matrix(edge, edge, True)
    along_x = gradient_matrix(2 * LANES, edge, False)
    lane = lax.broadcasted_iota(jnp.int32, (part, LANES), 1)
    ones_lane = jnp.where(lane == rest, 1.0, 0.0)
    land = lax.broadcasted_iota(jnp.int32, (rows, LANES), 0).astype(F32)
    first_row = (lax.axis_index("strip") * rows).astype(F32)
    if deep > used:
        keys[...] = jnp.full(keys.shape, -1.0, F32)
        base_out[used:, :] = jnp.zeros((deep - used, 2 * LANES), BF16)
    for slot, message in enumerate(messages):
        side = message[rows : rows + part, :].astype(F32)
        for p in range(count):
            halves = []
            for g in (2 * p, 2 * p + 1):
                left = message[g * part : (g + 1) * part, :].astype(F32)
                turned_side = pltpu.roll(side, (LANES - g * rest) % LANES, 1) if g else side
                halves.append(
                    jnp.concatenate([left, jnp.where(lane < rest, turned_side, ones_lane)], axis=1)
                )
            base = jnp.concatenate(halves, axis=0).astype(BF16)
            place = slice(slot * rows + p * edge, slot * rows + (p + 1) * edge)
            base_out[place, :] = base
            grad_y_out[place, :] = product(along_y, base).astype(BF16)
            grad_x_out[place, :] = product(base, along_x).astype(BF16)
        tail = message[rows + part :, :].astype(F32)
        key = tail[0:8] * 256.0 + tail[8:16] - first_row
        for j in range(0, rows, LANES):
            size = min(LANES, rows - j)
            line = key[j // LANES : j // LANES + 1, :size]
            keys[0:1, slot * rows + j : slot * rows + j + size] = line
    for j in range(0, deep, LANES):
        hit = land == keys[0:1, j : j + LANES]
        onehot[:, j : j + LANES] = jnp.where(hit, 1.0, 0.0).astype(BF16)


def align_rows(smooth, strip, count, edge, slot, base_in, grad_y_in, grad_x_in, stacked):
    mine = pltpu.roll(smooth, smooth.shape[1] - strip * count, 1)
    for p in range(count):
        place = slice(slot * count * edge + p * edge, slot * count * edge + (p + 1) * edge)
        smooth_y = jnp.broadcast_to(mine[0:1, p : p + 1], (edge, 2 * LANES)).astype(BF16)
        smooth_x = jnp.broadcast_to(mine[1:2, p : p + 1], (edge, 2 * LANES)).astype(BF16)
        change = smooth_y * grad_y_in[place, :] + smooth_x * grad_x_in[place, :]
        stacked[place, :] = base_in[place, :] + change


def averaged(total, edge):
    sums = jnp.transpose(total)
    return (sums[:edge] / jnp.maximum(sums[edge : edge + 1], 1.0)).astype(BF16)


def prepare_kernel(count, edge, slots, *refs):
    lay_out(refs[:slots], count, edge, refs[-1], *refs[-5:-1])


def render_kernel(count, edge, groups, *refs):
    prepared = refs[: 4 * len(groups)]
    smooth_a, smooth_b, out_ref = refs[4 * len(groups) : 4 * len(groups) + 3]
    stacks = refs[4 * len(groups) + 3 :]
    me = lax.axis_index("strip")
    smooth = smooth_a[...] + smooth_b[...]
    total = None
    for i, offsets in enumerate(groups):
        onehot, base, grad_y, grad_x = prepared[4 * i : 4 * i + 4]
        for slot, offset in enumerate(offsets):
            strip = jnp.bitwise_xor(me, offset)
            align_rows(smooth, strip, count, edge, slot, base, grad_y, grad_x, stacks[i])
        used = len(offsets) * count * edge
        if stacks[i].shape[0] > used:
            stacks[i][used:, :] = base[used:, :]
        part = product(onehot[...], stacks[i][...])
        total = part if total is None else total + part
    out_ref[...] = averaged(total, edge)


def render_all_kernel(
    count, edge, messages, smooth_ref, out_ref, onehot, base, grad_y, grad_x, keys, stacked
):
    rows = count * edge

    def step(i, total):
        lay_out([messages.at[i]], count, edge, keys, onehot, base, grad_y, grad_x)
        align_rows(smooth_ref[...], i, count, edge, 0, base, grad_y, grad_x, stacked)
        if stacked.shape[0] > rows:
            stacked[rows:, :] = base[rows:, :]
        return total + product(onehot[...], stacked[...])

    total = lax.fori_loop(0, messages.shape[0], step, jnp.zeros((rows, 2 * LANES), F32))
    out_ref[...] = averaged(total, edge)


def turned(block, axis, distance):
    size = lax.axis_size(axis)
    return lax.ppermute(block, axis, [(i, (i + distance) % size) for i in range(size)])


def swapped(block, offset):
    return lax.ppermute(
        block, "strip", [(i, i ^ offset) for i in range(lax.axis_size("strip"))]
    )


def on_device(image, peaks, row_source, row_weight, col_source, col_weight, owner, render_row):
    pixels = image[0]
    count, edge, _ = pixels.shape
    rows = count * edge
    sections, strips = lax.axis_size("sec"), lax.axis_size("strip")
    dft_cos, dft_sin = dft_tables(edge)
    length = message_rows(rows)
    wide = round_up(rows, LANES)

    inputs = (
        pixels,
        row_source[0],
        row_weight[0],
        col_source[0],
        col_weight[0],
        owner[0].reshape(1, rows),
        render_row,
    )
    message = call(
        base_kernel,
        jax.ShapeDtypeStruct((length, LANES), BF16),
        len(inputs),
        space=pltpu.HBM,
        scratch=[pltpu.VMEM(x.shape, x.dtype) for x in inputs]
        + [pltpu.VMEM((16, wide), F32), pltpu.SemaphoreType.DMA((len(inputs),))],
    )(*[pltpu.with_memory_space_constraint(x, pltpu.HBM) for x in inputs])
    prior_message = turned(message, "sec", 1)

    def table(*shape, kind=BF16):
        return jax.ShapeDtypeStruct(shape, kind)

    square = table(count, edge, edge, kind=F32)
    slim, tall = table(count, 16, edge), table(count, edge, LANES)
    *spectra, copied = call(
        spectrum_kernel,
        (square, square, slim, slim, tall, tall, table(length, LANES)),
        5,
    )(pixels, dft_cos, dft_sin, peaks[0], message)
    near, cross_re, cross_im = call(
        near_kernel,
        (table(8, LANES, kind=F32), table(count, edge, edge), table(count, edge, edge)),
        9,
    )(prior_message, *spectra[:2], dft_cos, dft_sin, *spectra[2:])

    surfaces = call(surface_kernel, (square,) * 3, 4)(cross_re, cross_im, dft_cos, dft_sin)

    def laid(slots):
        deep = round_up(slots * rows, LANES)
        return (table(rows, deep),) + (table(deep, 2 * LANES),) * 3

    def key_line(slots):
        return pltpu.VMEM((8, round_up(slots * rows, LANES)), F32)

    def stack(slots):
        return pltpu.VMEM((round_up(slots * rows, LANES), 2 * LANES), BF16)

    few = strips <= 8 and strips & (strips - 1) == 0
    order = [surfaces[0]]
    if few:
        offsets = [2 * k for k in range(strips // 2)]
        blocks = [copied]
        for offset in offsets[1:]:
            far = 1 << offset.bit_length() - 1
            blocks.append(swapped(copied, far) if offset == far else swapped(blocks[far // 2], offset - far))

        def prepared(group, after):
            return call(
                functools.partial(prepare_kernel, count, edge, len(group)),
                laid(len(group)),
                len(group) + 1,
                scratch=[key_line(len(group))],
            )(*group, after)

        early_side = prepared([copied, swapped(message, 1)], near)
        order.append(early_side[0])

    nears = [near] + [turned(near, "sec", k) for k in range(1, sections - 1)]
    patches_all = round_up(count * strips, LANES)
    smooth, prior = call(
        functools.partial(chain_kernel, count, len(nears)),
        (table(8, patches_all, kind=F32), table(8, LANES, kind=F32)),
        len(nears) + len(order),
    )(*nears, *order)
    corr_map, passed = call(map_kernel, (square, table(8, patches_all, kind=F32)), 5)(
        *surfaces, prior, smooth
    )

    rendered = table(edge, rows)
    if few:
        total = sum([swapped(smooth, offset) for offset in offsets[1:]], passed)
        late_side = prepared(blocks[1:] + [swapped(block, 1) for block in blocks[1:]], total)
        groups = [0, 1], offsets[1:] + [offset + 1 for offset in offsets[1:]]
        render = call(
            functools.partial(render_kernel, count, edge, groups),
            rendered,
            10,
            scratch=[stack(len(group)) for group in groups],
        )(*early_side, *late_side, total, swapped(total, 1))
    else:
        render = call(
            functools.partial(render_all_kernel, count, edge),
            rendered,
            2,
            scratch=[pltpu.VMEM(x.shape, x.dtype) for x in laid(1)] + [key_line(1), stack(1)],
            vmem=2 * strips * length * LANES * 2 + VMEM_BYTES,
        )(lax.all_gather(copied, "strip"), lax.psum(passed, "strip"))
    return (render.T[None], corr_map[None])


def solution(mesh):
    placed = (
        P("sec", "strip", None, None),
        P("sec", "strip", None),
        P("sec", "strip", None),
        P("sec", "strip", None),
        P("sec", "strip", None),
        P("sec", "strip", None),
        P("sec", "strip", None),
        P("sec", "strip"),
    )
    return jax.shard_map(
        on_device,
        mesh=mesh,
        in_specs=placed,
        out_specs=(P("sec", "strip", None), P("sec", "strip", None, None)),
        check_vma=False,
    )
```

```python
import functools

import jax
import jax.numpy as jnp
import numpy as np
from jax import lax
from jax.experimental import pallas as pl
from jax.experimental.pallas import tpu as pltpu
from jax.sharding import PartitionSpec as P

GC = 2
LANES = 128
TWO_PI = 2.0 * 3.141592653589793
F32 = jnp.float32
BF16 = jnp.bfloat16
VMEM_BYTES = 16 * 1024 * 1024


def product(left, right):
    return jnp.dot(left, right, preferred_element_type=F32)


def dft_tables(edge):
    positions = np.arange(edge, dtype=np.int32)
    phases = positions[:, None] * positions[None, :] % edge
    angles = phases.astype(np.float32) * np.float32(TWO_PI / edge)
    return jnp.asarray(np.cos(angles), BF16), jnp.asarray(np.sin(angles), BF16)


def round_up(size, unit):
    return -(-size // unit) * unit


def message_rows(rows):
    return rows + rows // 4 + 16


def call(kernel, out_shape, n_in, space=pltpu.VMEM, scratch=(), vmem=VMEM_BYTES, flops=1000000000):
    specs = [pl.BlockSpec(memory_space=space) for _ in range(n_in)]
    outs = jax.tree.map(lambda _: pl.BlockSpec(memory_space=pltpu.VMEM), out_shape)
    return pl.pallas_call(
        kernel,
        out_shape=out_shape,
        in_specs=specs,
        out_specs=outs,
        scratch_shapes=list(scratch),
        compiler_params=pltpu.CompilerParams(vmem_limit_bytes=vmem),
        cost_estimate=pl.CostEstimate(flops=flops, bytes_accessed=500000, transcendentals=0),
    )


def warp_matrix_t(source, weight, edge):
    spots = lax.broadcasted_iota(jnp.int32, (edge, edge), 0)
    following = jnp.where(source == edge - 1, 0, source + 1)
    first = jnp.where(spots == source, weight, 0.0)
    second = jnp.where(spots == following, 1.0 - weight, 0.0)
    return (first + second).astype(BF16)


def base_kernel(*refs):
    sources, out_ref, targets, sems = refs[:5], refs[5], refs[6:11], refs[11]
    copies = [
        pltpu.make_async_copy(source, target, sems.at[i])
        for i, (source, target) in enumerate(zip(sources, targets))
    ]
    for copy in copies:
        copy.start()
    image_ref, row_src, row_wt, col_src, col_wt = targets
    count, edge, _ = image_ref.shape
    rows = count * edge
    part = rows // 4
    for copy in copies[1:]:
        copy.wait()
    row_ts, col_ts = [], []
    for p in range(count):
        row_ts.append(warp_matrix_t(row_src[p : p + 1, :], row_wt[p : p + 1, :], edge))
        col_ts.append(warp_matrix_t(col_src[p : p + 1, :], col_wt[p : p + 1, :], edge))
    copies[0].wait()
    pieces = []
    for p in range(count):
        row_warped = lax.dot_general(
            row_ts[p], image_ref[p], (((0,), (0,)), ((), ())), preferred_element_type=F32
        ).astype(BF16)
        base = product(row_warped, col_ts[p])
        out_ref[p * edge : (p + 1) * edge, :] = base[:, :LANES].astype(BF16)
        right = base[:, LANES:]
        pieces += [right[:part], right[part:]]
    out_ref[rows : rows + part, :] = jnp.concatenate(pieces, axis=1).astype(BF16)


def landing_rows(owner_ref, target_ref, keys):
    rows = owner_ref.shape[1]
    keys[...] = jnp.full(keys.shape, -1.0, F32)
    key = owner_ref[...] * rows + target_ref[...]
    keys[0:1, 0:rows] = (key >> 8).astype(F32)
    keys[8:9, 0:rows] = (key & 255).astype(F32)
    wide = keys.shape[1] // LANES
    blank = jnp.full((8 - wide, LANES), -1.0, F32)
    lines = []
    for half in (0, 8):
        lines += [keys[half : half + 1, j * LANES : (j + 1) * LANES] for j in range(wide)]
        lines += [blank]
    return jnp.concatenate(lines, axis=0).astype(BF16)


def spectrum_of(pixels, dft_cos, dft_sin, count, edge):
    half_re = product(pixels, dft_cos).astype(BF16)
    half_im = (-product(pixels, dft_sin)).astype(BF16)
    spectra = []
    for p in range(count):
        h_re = half_re[p * edge : (p + 1) * edge]
        h_im = half_im[p * edge : (p + 1) * edge]
        spectra.append(
            (
                product(dft_cos, h_re) + product(dft_sin, h_im),
                product(dft_cos, h_im) - product(dft_sin, h_re),
            )
        )
    return spectra


def spectrum_kernel(
    image_ref,
    cos_ref,
    sin_ref,
    peaks_ref,
    base_ref,
    owner_ref,
    target_ref,
    re_ref,
    im_ref,
    cos_row,
    sin_row,
    cos_col,
    sin_col,
    message_ref,
    keys,
):
    count, edge, _ = image_ref.shape
    based = base_ref.shape[0]
    message_ref[0:based, :] = base_ref[...]
    message_ref[based:, :] = landing_rows(owner_ref, target_ref, keys)
    dft_cos, dft_sin = cos_ref[...], sin_ref[...]
    pixels = image_ref[...].reshape(count * edge, edge)
    spectra = spectrum_of(pixels, dft_cos, dft_sin, count, edge)
    for p, (s_re, s_im) in enumerate(spectra):
        re_ref[p] = s_re
        im_ref[p] = s_im

    def wrap(spot):
        return jnp.where(spot < 0, spot + edge, jnp.where(spot >= edge, spot - edge, spot))

    row = lax.broadcasted_iota(jnp.int32, (16, edge), 0)
    row_lane = lax.broadcasted_iota(jnp.int32, (16, edge), 1)
    col = lax.broadcasted_iota(jnp.int32, (edge, LANES), 0)
    col_lane = lax.broadcasted_iota(jnp.int32, (edge, LANES), 1)
    for p in range(count):
        spot = wrap(peaks_ref[p : p + 1, 0:1] + (row - 2))
        pick = jnp.where(jnp.logical_and(row < 5, row_lane == spot), 1.0, 0.0).astype(BF16)
        cos_row[p] = product(pick, dft_cos).astype(BF16)
        sin_row[p] = product(pick, dft_sin).astype(BF16)
        step = col_lane - (8 * p + 2)
        spot = wrap(peaks_ref[p : p + 1, 1:2] + step)
        near = jnp.logical_and(step >= -2, step <= 2)
        pick = jnp.where(jnp.logical_and(near, col == spot), 1.0, 0.0).astype(BF16)
        cos_col[p] = product(dft_cos, pick).astype(BF16)
        sin_col[p] = product(dft_sin, pick).astype(BF16)


def near_kernel(
    message_ref,
    im_re_ref,
    im_im_ref,
    cos_ref,
    sin_ref,
    cos_row,
    sin_row,
    cos_col,
    sin_col,
    near_ref,
    cross_re_ref,
    cross_im_ref,
):
    count, edge, _ = im_re_ref.shape
    rows = count * edge
    part = rows // 4
    rest = edge - LANES
    dft_cos, dft_sin = cos_ref[...], sin_ref[...]
    side = message_ref[rows : rows + part, :].astype(F32)
    groups = []
    for g in range(4):
        left = message_ref[g * part : (g + 1) * part, :].astype(F32)
        groups.append(jnp.concatenate([left, side[:, g * rest : (g + 1) * rest]], axis=1))
    pixels = jnp.concatenate(groups, axis=0)
    pixels = jnp.where(lax.axis_index("sec") > 0, pixels, 0.0).astype(BF16)
    spectra = spectrum_of(pixels, dft_cos, dft_sin, count, edge)
    cross = []
    for p, (ref_re, ref_im) in enumerate(spectra):
        img_re, img_im = im_re_ref[p], im_im_ref[p]
        cross_re = (ref_re * img_re + ref_im * img_im).astype(BF16)
        cross_im = (ref_im * img_re - ref_re * img_im).astype(BF16)
        cross.append((cross_re, cross_im))
    back = []
    for p, (cross_re, cross_im) in enumerate(cross):
        back_re = (product(cross_re, cos_col[p]) - product(cross_im, sin_col[p])).astype(BF16)
        back_im = (product(cross_re, sin_col[p]) + product(cross_im, cos_col[p])).astype(BF16)
        back.append((back_re, back_im))
    total = None
    for p, (back_re, back_im) in enumerate(back):
        near = product(cos_row[p], back_re) - product(sin_row[p], back_im)
        total = near if total is None else total + near
    for p, (cross_re, cross_im) in enumerate(cross):
        cross_re_ref[p] = cross_re
        cross_im_ref[p] = cross_im
    near_ref[...] = total[0:8] * (1.0 / (edge * edge))


def chain_kernel(count, steps, *refs):
    near_refs, (smooth_ref, prior_ref) = refs[:steps], refs[-2:]
    section = lax.axis_index("sec")
    strip = lax.axis_index("strip")
    row = lax.broadcasted_iota(jnp.int32, (8, LANES), 0)
    lane = lax.broadcasted_iota(jnp.int32, (8, LANES), 1)

    def spread(values):
        tile = jnp.broadcast_to(values[0], (8, LANES))
        for p in range(1, count):
            tile = jnp.where(lane >= 8 * p, values[p], tile)
        return tile

    zeros = [jnp.zeros((1, 1), F32)] * count
    smooth_y, smooth_x = zeros, zeros
    for back in range(steps - 1, -1, -1):
        prior_y, prior_x = smooth_y, smooth_x
        near = near_refs[back][...]
        grad_y = 0.5 * (pltpu.roll(near, 7, 0) - pltpu.roll(near, 1, 0))
        grad_x = 0.5 * (pltpu.roll(near, LANES - 1, 1) - pltpu.roll(near, 1, 1))
        corr = near + spread(prior_y) * grad_y + spread(prior_x) * grad_x
        size = jnp.abs(corr)
        below, above = pltpu.roll(corr, 7, 0), pltpu.roll(corr, 1, 0)
        right, left = pltpu.roll(corr, LANES - 1, 1), pltpu.roll(corr, 1, 1)
        flow_y = (below - above) / (jnp.abs(below) + size + jnp.abs(above) + 1.0)
        flow_x = (right - left) / (jnp.abs(right) + size + jnp.abs(left) + 1.0)

        def picked(flow):
            values = []
            for p in range(count):
                here = jnp.logical_and(row == 2, lane == 8 * p + 2)
                spot = jnp.where(here, flow, 0.0)
                values.append(jnp.sum(jnp.sum(spot, axis=1, keepdims=True), axis=0, keepdims=True))
            smooth = []
            for p in range(count):
                total = 0.5 * values[p]
                if p % GC > 0:
                    total = total + 0.25 * values[p - 1]
                if p % GC < GC - 1:
                    total = total + 0.25 * values[p + 1]
                smooth.append(jnp.where(section - back > 0, total, 0.0))
            return smooth

        smooth_y, smooth_x = picked(flow_y), picked(flow_x)

    def laid(values_y, values_x, shape, first):
        out_row = lax.broadcasted_iota(jnp.int32, shape, 0)
        out_lane = lax.broadcasted_iota(jnp.int32, shape, 1)
        tile = jnp.zeros(shape, F32)
        for p in range(count):
            pair = jnp.where(out_row == 0, values_y[p], values_x[p])
            here = jnp.logical_and(out_lane == first + p, out_row < 2)
            tile = jnp.where(here, pair, tile)
        return tile

    smooth_ref[...] = laid(smooth_y, smooth_x, smooth_ref.shape, strip * count)
    prior_ref[...] = laid(prior_y, prior_x, prior_ref.shape, 0)


def surface_kernel(cross_re_ref, cross_im_ref, cos_ref, sin_ref, corr_ref, grad_y_ref, grad_x_ref):
    count, edge, _ = cross_re_ref.shape
    dft_cos, dft_sin = cos_ref[...], sin_ref[...]
    for p in range(count):
        cross_re, cross_im = cross_re_ref[p], cross_im_ref[p]
        back_re = (product(cross_re, dft_cos) - product(cross_im, dft_sin)).astype(BF16)
        back_im = (product(cross_re, dft_sin) + product(cross_im, dft_cos)).astype(BF16)
        corr = product(dft_cos, back_re) - product(dft_sin, back_im)
        corr = corr * (1.0 / (edge * edge * edge))
        corr_ref[p] = corr
        grad_y_ref[p] = 0.5 * (jnp.roll(corr, -1, axis=0) - jnp.roll(corr, 1, axis=0))
        grad_x_ref[p] = 0.5 * (jnp.roll(corr, -1, axis=1) - jnp.roll(corr, 1, axis=1))


def map_kernel(corr_ref, grad_y_ref, grad_x_ref, prior_ref, smooth_ref, out_ref, passed_ref):
    passed_ref[...] = smooth_ref[...]
    for p in range(corr_ref.shape[0]):
        smooth_y = prior_ref[0:1, p : p + 1]
        smooth_x = prior_ref[1:2, p : p + 1]
        out_ref[p] = corr_ref[p] + smooth_y * grad_y_ref[p] + smooth_x * grad_x_ref[p]


def gradient_matrix(size, edge, up):
    row = lax.broadcasted_iota(jnp.int32, (size, size), 0)
    col = lax.broadcasted_iota(jnp.int32, (size, size), 1)
    out, source = (row, col) if up else (col, row)
    following = jnp.where(out == edge - 1, 0, out + 1)
    before = jnp.where(out == 0, edge - 1, out - 1)
    inside = out < edge
    plus = jnp.where(jnp.logical_and(inside, source == following), 0.5, 0.0)
    minus = jnp.where(jnp.logical_and(inside, source == before), 0.5, 0.0)
    return (plus - minus).astype(BF16)


def lay_out(messages, count, edge, keys, onehot, base_out, grad_y_out, grad_x_out):
    rows = count * edge
    part = rows // 4
    rest = edge - LANES
    deep = onehot.shape[1]
    used = len(messages) * rows
    along_y = gradient_matrix(edge, edge, True)
    along_x = gradient_matrix(2 * LANES, edge, False)
    lane = lax.broadcasted_iota(jnp.int32, (part, LANES), 1)
    ones_lane = jnp.where(lane == rest, 1.0, 0.0)
    land = lax.broadcasted_iota(jnp.int32, (rows, LANES), 0).astype(F32)
    first_row = (lax.axis_index("strip") * rows).astype(F32)
    if deep > used:
        keys[...] = jnp.full(keys.shape, -1.0, F32)
        base_out[used:, :] = jnp.zeros((deep - used, 2 * LANES), BF16)
    for slot, message in enumerate(messages):
        side = message[rows : rows + part, :].astype(F32)
        for p in range(count):
            halves = []
            for g in (2 * p, 2 * p + 1):
                left = message[g * part : (g + 1) * part, :].astype(F32)
                turned_side = pltpu.roll(side, (LANES - g * rest) % LANES, 1) if g else side
                halves.append(
                    jnp.concatenate([left, jnp.where(lane < rest, turned_side, ones_lane)], axis=1)
                )
            base = jnp.concatenate(halves, axis=0).astype(BF16)
            place = slice(slot * rows + p * edge, slot * rows + (p + 1) * edge)
            base_out[place, :] = base
            grad_y_out[place, :] = product(along_y, base).astype(BF16)
            grad_x_out[place, :] = product(base, along_x).astype(BF16)
        tail = message[rows + part :, :].astype(F32)
        key = tail[0:8] * 256.0 + tail[8:16] - first_row
        for j in range(0, rows, LANES):
            size = min(LANES, rows - j)
            line = key[j // LANES : j // LANES + 1, :size]
            keys[0:1, slot * rows + j : slot * rows + j + size] = line
    for j in range(0, deep, LANES):
        hit = land == keys[0:1, j : j + LANES]
        onehot[:, j : j + LANES] = jnp.where(hit, 1.0, 0.0).astype(BF16)


def align_rows(smooth, strip, count, edge, slot, base_in, grad_y_in, grad_x_in, stacked):
    mine = pltpu.roll(smooth, smooth.shape[1] - strip * count, 1)
    for p in range(count):
        place = slice(slot * count * edge + p * edge, slot * count * edge + (p + 1) * edge)
        smooth_y = jnp.broadcast_to(mine[0:1, p : p + 1], (edge, 2 * LANES)).astype(BF16)
        smooth_x = jnp.broadcast_to(mine[1:2, p : p + 1], (edge, 2 * LANES)).astype(BF16)
        change = smooth_y * grad_y_in[place, :] + smooth_x * grad_x_in[place, :]
        stacked[place, :] = base_in[place, :] + change


def averaged(total, edge):
    sums = jnp.transpose(total)
    return (sums[:edge] / jnp.maximum(sums[edge : edge + 1], 1.0)).astype(BF16)


def prepare_kernel(count, edge, slots, *refs):
    lay_out(refs[:slots], count, edge, refs[-1], *refs[-5:-1])


def render_kernel(count, edge, groups, *refs):
    prepared = refs[: 4 * len(groups)]
    smooth_a, smooth_b, out_ref = refs[4 * len(groups) : 4 * len(groups) + 3]
    stacks = refs[4 * len(groups) + 3 :]
    me = lax.axis_index("strip")
    smooth = smooth_a[...] + smooth_b[...]
    total = None
    for i, offsets in enumerate(groups):
        onehot, base, grad_y, grad_x = prepared[4 * i : 4 * i + 4]
        for slot, offset in enumerate(offsets):
            strip = jnp.bitwise_xor(me, offset)
            align_rows(smooth, strip, count, edge, slot, base, grad_y, grad_x, stacks[i])
        used = len(offsets) * count * edge
        if stacks[i].shape[0] > used:
            stacks[i][used:, :] = base[used:, :]
        part = product(onehot[...], stacks[i][...])
        total = part if total is None else total + part
    out_ref[...] = averaged(total, edge)


def render_all_kernel(
    count, edge, messages, smooth_ref, out_ref, onehot, base, grad_y, grad_x, keys, stacked
):
    rows = count * edge

    def step(i, total):
        lay_out([messages.at[i]], count, edge, keys, onehot, base, grad_y, grad_x)
        align_rows(smooth_ref[...], i, count, edge, 0, base, grad_y, grad_x, stacked)
        if stacked.shape[0] > rows:
            stacked[rows:, :] = base[rows:, :]
        return total + product(onehot[...], stacked[...])

    total = lax.fori_loop(0, messages.shape[0], step, jnp.zeros((rows, 2 * LANES), F32))
    out_ref[...] = averaged(total, edge)


def turned(block, axis, distance):
    size = lax.axis_size(axis)
    return lax.ppermute(block, axis, [(i, (i + distance) % size) for i in range(size)])


def swapped(block, offset):
    return lax.ppermute(
        block, "strip", [(i, i ^ offset) for i in range(lax.axis_size("strip"))]
    )


def on_device(image, peaks, row_source, row_weight, col_source, col_weight, owner, render_row):
    pixels = image[0]
    count, edge, _ = pixels.shape
    rows = count * edge
    sections, strips = lax.axis_size("sec"), lax.axis_size("strip")
    dft_cos, dft_sin = dft_tables(edge)
    length = message_rows(rows)
    wide = round_up(rows, LANES)

    inputs = (pixels, row_source[0], row_weight[0], col_source[0], col_weight[0])
    base = call(
        base_kernel,
        jax.ShapeDtypeStruct((length - 16, LANES), BF16),
        len(inputs),
        space=pltpu.HBM,
        scratch=[pltpu.VMEM(x.shape, x.dtype) for x in inputs]
        + [pltpu.SemaphoreType.DMA((len(inputs),))],
    )(*[pltpu.with_memory_space_constraint(x, pltpu.HBM) for x in inputs])
    prior_base = turned(base, "sec", 1)

    def table(*shape, kind=BF16):
        return jax.ShapeDtypeStruct(shape, kind)

    square = table(count, edge, edge, kind=F32)
    slim, tall = table(count, 16, edge), table(count, edge, LANES)
    *spectra, message = call(
        spectrum_kernel,
        (square, square, slim, slim, tall, tall, table(length, LANES)),
        7,
        scratch=[pltpu.VMEM((16, wide), F32)],
    )(pixels, dft_cos, dft_sin, peaks[0], base, owner[0].reshape(1, rows), render_row)
    near, cross_re, cross_im = call(
        near_kernel,
        (table(8, LANES, kind=F32), table(count, edge, edge), table(count, edge, edge)),
        9,
    )(prior_base, *spectra[:2], dft_cos, dft_sin, *spectra[2:])

    surfaces = call(surface_kernel, (square,) * 3, 4)(cross_re, cross_im, dft_cos, dft_sin)

    def laid(slots):
        deep = round_up(slots * rows, LANES)
        return (table(rows, deep),) + (table(deep, 2 * LANES),) * 3

    def key_line(slots):
        return pltpu.VMEM((8, round_up(slots * rows, LANES)), F32)

    def stack(slots):
        return pltpu.VMEM((round_up(slots * rows, LANES), 2 * LANES), BF16)

    few = strips == 8
    order = [surfaces[0]]
    if few:
        offsets = [2 * k for k in range(strips // 2)]
        blocks = [message]
        for offset in offsets[1:]:
            far = 1 << offset.bit_length() - 1
            blocks.append(swapped(message, far) if offset == far else swapped(blocks[far // 2], offset - far))

        def prepared(group, after):
            return call(
                functools.partial(prepare_kernel, count, edge, len(group)),
                laid(len(group)),
                len(group) + 1,
                scratch=[key_line(len(group))],
            )(*group, after)

        early_side = prepared([message, swapped(message, 1)], near)
        order.append(early_side[0])

    nears = [near] + [turned(near, "sec", k) for k in range(1, sections - 1)]
    patches_all = round_up(count * strips, LANES)
    smooth, prior = call(
        functools.partial(chain_kernel, count, len(nears)),
        (table(8, patches_all, kind=F32), table(8, LANES, kind=F32)),
        len(nears) + len(order),
    )(*nears, *order)
    corr_map, passed = call(map_kernel, (square, table(8, patches_all, kind=F32)), 5)(
        *surfaces, prior, smooth
    )

    rendered = table(edge, rows)
    if few:
        total = sum([swapped(smooth, offset) for offset in offsets[1:]], passed)
        late_side = prepared(blocks[1:] + [swapped(block, 1) for block in blocks[1:]], total)
        groups = [0, 1], offsets[1:] + [offset + 1 for offset in offsets[1:]]
        render = call(
            functools.partial(render_kernel, count, edge, groups),
            rendered,
            10,
            scratch=[stack(len(group)) for group in groups],
        )(*early_side, *late_side, total, swapped(total, 1))
    else:
        render = call(
            functools.partial(render_all_kernel, count, edge),
            rendered,
            2,
            scratch=[pltpu.VMEM(x.shape, x.dtype) for x in laid(1)] + [key_line(1), stack(1)],
            vmem=2 * strips * length * LANES * 2 + VMEM_BYTES,
        )(lax.all_gather(message, "strip"), lax.psum(passed, "strip"))
    return (render.T[None], corr_map[None])


def solution(mesh):
    placed = (
        P("sec", "strip", None, None),
        P("sec", "strip", None),
        P("sec", "strip", None),
        P("sec", "strip", None),
        P("sec", "strip", None),
        P("sec", "strip", None),
        P("sec", "strip", None),
        P("sec", "strip"),
    )
    return jax.shard_map(
        on_device,
        mesh=mesh,
        in_specs=placed,
        out_specs=(P("sec", "strip", None), P("sec", "strip", None, None)),
        check_vma=False,
    )
```

```python
import functools

import jax
import jax.numpy as jnp
import numpy as np
from jax import lax
from jax.experimental import pallas as pl
from jax.experimental.pallas import tpu as pltpu
from jax.sharding import PartitionSpec as P

GC = 2
LANES = 128
TWO_PI = 2.0 * 3.141592653589793
F32 = jnp.float32
BF16 = jnp.bfloat16
VMEM_BYTES = 16 * 1024 * 1024


def product(left, right):
    return jnp.dot(left, right, preferred_element_type=F32)


def dft_tables(edge):
    positions = np.arange(edge, dtype=np.int32)
    phases = positions[:, None] * positions[None, :] % edge
    angles = phases.astype(np.float32) * np.float32(TWO_PI / edge)
    return jnp.asarray(np.cos(angles), BF16), jnp.asarray(np.sin(angles), BF16)


def round_up(size, unit):
    return -(-size // unit) * unit


def message_rows(rows):
    return rows + rows // 4 + 16


def call(kernel, out_shape, n_in, space=pltpu.VMEM, scratch=(), vmem=VMEM_BYTES, flops=1000000000):
    specs = [pl.BlockSpec(memory_space=space) for _ in range(n_in)]
    outs = jax.tree.map(lambda _: pl.BlockSpec(memory_space=pltpu.VMEM), out_shape)
    return pl.pallas_call(
        kernel,
        out_shape=out_shape,
        in_specs=specs,
        out_specs=outs,
        scratch_shapes=list(scratch),
        compiler_params=pltpu.CompilerParams(vmem_limit_bytes=vmem),
        cost_estimate=pl.CostEstimate(flops=flops, bytes_accessed=500000, transcendentals=0),
    )


def warp_matrix_t(source, weight, edge):
    spots = lax.broadcasted_iota(jnp.int32, (edge, edge), 0)
    following = jnp.where(source == edge - 1, 0, source + 1)
    first = jnp.where(spots == source, weight, 0.0)
    second = jnp.where(spots == following, 1.0 - weight, 0.0)
    return (first + second).astype(BF16)


def base_kernel(*refs):
    sources, out_ref, targets, sems = refs[:5], refs[5], refs[6:11], refs[11]
    copies = [
        pltpu.make_async_copy(source, target, sems.at[i])
        for i, (source, target) in enumerate(zip(sources, targets))
    ]
    for copy in copies:
        copy.start()
    image_ref, row_src, row_wt, col_src, col_wt = targets
    count, edge, _ = image_ref.shape
    rows = count * edge
    part = rows // 4
    for copy in copies[1:]:
        copy.wait()
    row_ts, col_ts = [], []
    for p in range(count):
        row_ts.append(warp_matrix_t(row_src[p : p + 1, :], row_wt[p : p + 1, :], edge))
        col_ts.append(warp_matrix_t(col_src[p : p + 1, :], col_wt[p : p + 1, :], edge))
    copies[0].wait()
    pieces = []
    for p in range(count):
        row_warped = lax.dot_general(
            row_ts[p], image_ref[p], (((0,), (0,)), ((), ())), preferred_element_type=F32
        ).astype(BF16)
        base = product(row_warped, col_ts[p])
        out_ref[p * edge : (p + 1) * edge, :] = base[:, :LANES].astype(BF16)
        right = base[:, LANES:]
        pieces += [right[:part], right[part:]]
    out_ref[rows : rows + part, :] = jnp.concatenate(pieces, axis=1).astype(BF16)


def landing_rows(owner_ref, target_ref, keys):
    rows = owner_ref.shape[1]
    keys[...] = jnp.full(keys.shape, -1.0, F32)
    key = owner_ref[...] * rows + target_ref[...]
    keys[0:1, 0:rows] = (key >> 8).astype(F32)
    keys[8:9, 0:rows] = (key & 255).astype(F32)
    wide = keys.shape[1] // LANES
    blank = jnp.full((8 - wide, LANES), -1.0, F32)
    lines = []
    for half in (0, 8):
        lines += [keys[half : half + 1, j * LANES : (j + 1) * LANES] for j in range(wide)]
        lines += [blank]
    return jnp.concatenate(lines, axis=0).astype(BF16)


def spectrum_of(pixels, dft_cos, dft_sin, count, edge):
    half_re = product(pixels, dft_cos).astype(BF16)
    half_im = (-product(pixels, dft_sin)).astype(BF16)
    spectra = []
    for p in range(count):
        h_re = half_re[p * edge : (p + 1) * edge]
        h_im = half_im[p * edge : (p + 1) * edge]
        spectra.append(
            (
                product(dft_cos, h_re) + product(dft_sin, h_im),
                product(dft_cos, h_im) - product(dft_sin, h_re),
            )
        )
    return spectra


def spectrum_kernel(
    image_ref,
    cos_ref,
    sin_ref,
    peaks_ref,
    base_ref,
    owner_ref,
    target_ref,
    re_ref,
    im_ref,
    cos_row,
    sin_row,
    cos_col,
    sin_col,
    message_ref,
    keys,
):
    count, edge, _ = image_ref.shape
    based = base_ref.shape[0]
    message_ref[0:based, :] = base_ref[...]
    message_ref[based:, :] = landing_rows(owner_ref, target_ref, keys)
    dft_cos, dft_sin = cos_ref[...], sin_ref[...]
    def wrap(spot):
        return jnp.where(spot < 0, spot + edge, jnp.where(spot >= edge, spot - edge, spot))

    row = lax.broadcasted_iota(jnp.int32, (16, edge), 0)
    row_lane = lax.broadcasted_iota(jnp.int32, (16, edge), 1)
    col = lax.broadcasted_iota(jnp.int32, (edge, LANES), 0)
    col_lane = lax.broadcasted_iota(jnp.int32, (edge, LANES), 1)
    for p in range(count):
        spot = wrap(peaks_ref[p : p + 1, 0:1] + (row - 2))
        pick = jnp.where(jnp.logical_and(row < 5, row_lane == spot), 1.0, 0.0).astype(BF16)
        cos_row[p] = product(pick, dft_cos).astype(BF16)
        sin_row[p] = product(pick, dft_sin).astype(BF16)
        step = col_lane - (8 * p + 2)
        spot = wrap(peaks_ref[p : p + 1, 1:2] + step)
        near = jnp.logical_and(step >= -2, step <= 2)
        pick = jnp.where(jnp.logical_and(near, col == spot), 1.0, 0.0).astype(BF16)
        cos_col[p] = product(dft_cos, pick).astype(BF16)
        sin_col[p] = product(dft_sin, pick).astype(BF16)
    pixels = image_ref[...].reshape(count * edge, edge)
    spectra = spectrum_of(pixels, dft_cos, dft_sin, count, edge)
    for p, (s_re, s_im) in enumerate(spectra):
        re_ref[p] = s_re
        im_ref[p] = s_im


def near_kernel(
    message_ref,
    im_re_ref,
    im_im_ref,
    cos_ref,
    sin_ref,
    cos_row,
    sin_row,
    cos_col,
    sin_col,
    near_ref,
    cross_re_ref,
    cross_im_ref,
):
    count, edge, _ = im_re_ref.shape
    rows = count * edge
    part = rows // 4
    rest = edge - LANES
    dft_cos, dft_sin = cos_ref[...], sin_ref[...]
    side = message_ref[rows : rows + part, :].astype(F32)
    groups = []
    for g in range(4):
        left = message_ref[g * part : (g + 1) * part, :].astype(F32)
        groups.append(jnp.concatenate([left, side[:, g * rest : (g + 1) * rest]], axis=1))
    pixels = jnp.concatenate(groups, axis=0)
    pixels = jnp.where(lax.axis_index("sec") > 0, pixels, 0.0).astype(BF16)
    spectra = spectrum_of(pixels, dft_cos, dft_sin, count, edge)
    cross = []
    for p, (ref_re, ref_im) in enumerate(spectra):
        img_re, img_im = im_re_ref[p], im_im_ref[p]
        cross_re = (ref_re * img_re + ref_im * img_im).astype(BF16)
        cross_im = (ref_im * img_re - ref_re * img_im).astype(BF16)
        cross.append((cross_re, cross_im))
    back = []
    for p, (cross_re, cross_im) in enumerate(cross):
        back_re = (product(cross_re, cos_col[p]) - product(cross_im, sin_col[p])).astype(BF16)
        back_im = (product(cross_re, sin_col[p]) + product(cross_im, cos_col[p])).astype(BF16)
        back.append((back_re, back_im))
    total = None
    for p, (back_re, back_im) in enumerate(back):
        near = product(cos_row[p], back_re) - product(sin_row[p], back_im)
        total = near if total is None else total + near
    for p, (cross_re, cross_im) in enumerate(cross):
        cross_re_ref[p] = cross_re
        cross_im_ref[p] = cross_im
    near_ref[...] = total[0:8] * (1.0 / (edge * edge))


def chain_kernel(count, steps, *refs):
    near_refs, (smooth_ref, prior_ref) = refs[:steps], refs[-2:]
    section = lax.axis_index("sec")
    strip = lax.axis_index("strip")
    row = lax.broadcasted_iota(jnp.int32, (8, LANES), 0)
    lane = lax.broadcasted_iota(jnp.int32, (8, LANES), 1)

    def spread(values):
        tile = jnp.broadcast_to(values[0], (8, LANES))
        for p in range(1, count):
            tile = jnp.where(lane >= 8 * p, values[p], tile)
        return tile

    zeros = [jnp.zeros((1, 1), F32)] * count
    smooth_y, smooth_x = zeros, zeros
    for back in range(steps - 1, -1, -1):
        prior_y, prior_x = smooth_y, smooth_x
        near = near_refs[back][...]
        grad_y = 0.5 * (pltpu.roll(near, 7, 0) - pltpu.roll(near, 1, 0))
        grad_x = 0.5 * (pltpu.roll(near, LANES - 1, 1) - pltpu.roll(near, 1, 1))
        corr = near + spread(prior_y) * grad_y + spread(prior_x) * grad_x
        size = jnp.abs(corr)
        below, above = pltpu.roll(corr, 7, 0), pltpu.roll(corr, 1, 0)
        right, left = pltpu.roll(corr, LANES - 1, 1), pltpu.roll(corr, 1, 1)
        flow_y = (below - above) / (jnp.abs(below) + size + jnp.abs(above) + 1.0)
        flow_x = (right - left) / (jnp.abs(right) + size + jnp.abs(left) + 1.0)

        def picked(flow):
            values = []
            for p in range(count):
                here = jnp.logical_and(row == 2, lane == 8 * p + 2)
                spot = jnp.where(here, flow, 0.0)
                values.append(jnp.sum(jnp.sum(spot, axis=1, keepdims=True), axis=0, keepdims=True))
            smooth = []
            for p in range(count):
                total = 0.5 * values[p]
                if p % GC > 0:
                    total = total + 0.25 * values[p - 1]
                if p % GC < GC - 1:
                    total = total + 0.25 * values[p + 1]
                smooth.append(jnp.where(section - back > 0, total, 0.0))
            return smooth

        smooth_y, smooth_x = picked(flow_y), picked(flow_x)

    def laid(values_y, values_x, shape, first):
        out_row = lax.broadcasted_iota(jnp.int32, shape, 0)
        out_lane = lax.broadcasted_iota(jnp.int32, shape, 1)
        tile = jnp.zeros(shape, F32)
        for p in range(count):
            pair = jnp.where(out_row == 0, values_y[p], values_x[p])
            here = jnp.logical_and(out_lane == first + p, out_row < 2)
            tile = jnp.where(here, pair, tile)
        return tile

    smooth_ref[...] = laid(smooth_y, smooth_x, smooth_ref.shape, strip * count)
    prior_ref[...] = laid(prior_y, prior_x, prior_ref.shape, 0)


def surface_kernel(cross_re_ref, cross_im_ref, cos_ref, sin_ref, corr_ref, grad_y_ref, grad_x_ref):
    count, edge, _ = cross_re_ref.shape
    dft_cos, dft_sin = cos_ref[...], sin_ref[...]
    for p in range(count):
        cross_re, cross_im = cross_re_ref[p], cross_im_ref[p]
        back_re = (product(cross_re, dft_cos) - product(cross_im, dft_sin)).astype(BF16)
        back_im = (product(cross_re, dft_sin) + product(cross_im, dft_cos)).astype(BF16)
        corr = product(dft_cos, back_re) - product(dft_sin, back_im)
        corr = corr * (1.0 / (edge * edge * edge))
        corr_ref[p] = corr
        grad_y_ref[p] = 0.5 * (jnp.roll(corr, -1, axis=0) - jnp.roll(corr, 1, axis=0))
        grad_x_ref[p] = 0.5 * (jnp.roll(corr, -1, axis=1) - jnp.roll(corr, 1, axis=1))


def map_kernel(corr_ref, grad_y_ref, grad_x_ref, prior_ref, smooth_ref, out_ref, passed_ref):
    passed_ref[...] = smooth_ref[...]
    for p in range(corr_ref.shape[0]):
        smooth_y = prior_ref[0:1, p : p + 1]
        smooth_x = prior_ref[1:2, p : p + 1]
        out_ref[p] = corr_ref[p] + smooth_y * grad_y_ref[p] + smooth_x * grad_x_ref[p]


def gradient_matrix(size, edge, up):
    row = lax.broadcasted_iota(jnp.int32, (size, size), 0)
    col = lax.broadcasted_iota(jnp.int32, (size, size), 1)
    out, source = (row, col) if up else (col, row)
    following = jnp.where(out == edge - 1, 0, out + 1)
    before = jnp.where(out == 0, edge - 1, out - 1)
    inside = out < edge
    plus = jnp.where(jnp.logical_and(inside, source == following), 0.5, 0.0)
    minus = jnp.where(jnp.logical_and(inside, source == before), 0.5, 0.0)
    return (plus - minus).astype(BF16)


def lay_out(messages, count, edge, keys, onehot, base_out, grad_y_out, grad_x_out):
    rows = count * edge
    part = rows // 4
    rest = edge - LANES
    deep = onehot.shape[1]
    used = len(messages) * rows
    along_y = gradient_matrix(edge, edge, True)
    along_x = gradient_matrix(2 * LANES, edge, False)
    lane = lax.broadcasted_iota(jnp.int32, (part, LANES), 1)
    ones_lane = jnp.where(lane == rest, 1.0, 0.0)
    land = lax.broadcasted_iota(jnp.int32, (rows, LANES), 0).astype(F32)
    first_row = (lax.axis_index("strip") * rows).astype(F32)
    if deep > used:
        keys[...] = jnp.full(keys.shape, -1.0, F32)
        base_out[used:, :] = jnp.zeros((deep - used, 2 * LANES), BF16)
    for slot, message in enumerate(messages):
        side = message[rows : rows + part, :].astype(F32)
        for p in range(count):
            halves = []
            for g in (2 * p, 2 * p + 1):
                left = message[g * part : (g + 1) * part, :].astype(F32)
                turned_side = pltpu.roll(side, (LANES - g * rest) % LANES, 1) if g else side
                halves.append(
                    jnp.concatenate([left, jnp.where(lane < rest, turned_side, ones_lane)], axis=1)
                )
            base = jnp.concatenate(halves, axis=0).astype(BF16)
            place = slice(slot * rows + p * edge, slot * rows + (p + 1) * edge)
            base_out[place, :] = base
            grad_y_out[place, :] = product(along_y, base).astype(BF16)
            grad_x_out[place, :] = product(base, along_x).astype(BF16)
        tail = message[rows + part :, :].astype(F32)
        key = tail[0:8] * 256.0 + tail[8:16] - first_row
        for j in range(0, rows, LANES):
            size = min(LANES, rows - j)
            line = key[j // LANES : j // LANES + 1, :size]
            keys[0:1, slot * rows + j : slot * rows + j + size] = line
    for j in range(0, deep, LANES):
        hit = land == keys[0:1, j : j + LANES]
        onehot[:, j : j + LANES] = jnp.where(hit, 1.0, 0.0).astype(BF16)


def align_rows(smooth, strip, count, edge, slot, base_in, grad_y_in, grad_x_in, stacked):
    mine = pltpu.roll(smooth, smooth.shape[1] - strip * count, 1)
    for p in range(count):
        place = slice(slot * count * edge + p * edge, slot * count * edge + (p + 1) * edge)
        smooth_y = jnp.broadcast_to(mine[0:1, p : p + 1], (edge, 2 * LANES)).astype(BF16)
        smooth_x = jnp.broadcast_to(mine[1:2, p : p + 1], (edge, 2 * LANES)).astype(BF16)
        change = smooth_y * grad_y_in[place, :] + smooth_x * grad_x_in[place, :]
        stacked[place, :] = base_in[place, :] + change


def averaged(total, edge):
    sums = jnp.transpose(total)
    return (sums[:edge] / jnp.maximum(sums[edge : edge + 1], 1.0)).astype(BF16)


def prepare_kernel(count, edge, slots, *refs):
    lay_out(refs[:slots], count, edge, refs[-1], *refs[-5:-1])


def render_kernel(count, edge, groups, *refs):
    prepared = refs[: 4 * len(groups)]
    smooth_a, smooth_b, out_ref = refs[4 * len(groups) : 4 * len(groups) + 3]
    stacks = refs[4 * len(groups) + 3 :]
    me = lax.axis_index("strip")
    smooth = smooth_a[...] + smooth_b[...]
    total = None
    for i, offsets in enumerate(groups):
        onehot, base, grad_y, grad_x = prepared[4 * i : 4 * i + 4]
        for slot, offset in enumerate(offsets):
            strip = jnp.bitwise_xor(me, offset)
            align_rows(smooth, strip, count, edge, slot, base, grad_y, grad_x, stacks[i])
        used = len(offsets) * count * edge
        if stacks[i].shape[0] > used:
            stacks[i][used:, :] = base[used:, :]
        part = product(onehot[...], stacks[i][...])
        total = part if total is None else total + part
    out_ref[...] = averaged(total, edge)


def render_all_kernel(
    count, edge, messages, smooth_ref, out_ref, onehot, base, grad_y, grad_x, keys, stacked
):
    rows = count * edge

    def step(i, total):
        lay_out([messages.at[i]], count, edge, keys, onehot, base, grad_y, grad_x)
        align_rows(smooth_ref[...], i, count, edge, 0, base, grad_y, grad_x, stacked)
        if stacked.shape[0] > rows:
            stacked[rows:, :] = base[rows:, :]
        return total + product(onehot[...], stacked[...])

    total = lax.fori_loop(0, messages.shape[0], step, jnp.zeros((rows, 2 * LANES), F32))
    out_ref[...] = averaged(total, edge)


def turned(block, axis, distance):
    size = lax.axis_size(axis)
    return lax.ppermute(block, axis, [(i, (i + distance) % size) for i in range(size)])


def swapped(block, offset):
    return lax.ppermute(
        block, "strip", [(i, i ^ offset) for i in range(lax.axis_size("strip"))]
    )


def on_device(image, peaks, row_source, row_weight, col_source, col_weight, owner, render_row):
    pixels = image[0]
    count, edge, _ = pixels.shape
    rows = count * edge
    sections, strips = lax.axis_size("sec"), lax.axis_size("strip")
    dft_cos, dft_sin = dft_tables(edge)
    length = message_rows(rows)
    wide = round_up(rows, LANES)

    inputs = (pixels, row_source[0], row_weight[0], col_source[0], col_weight[0])
    base = call(
        base_kernel,
        jax.ShapeDtypeStruct((length - 16, LANES), BF16),
        len(inputs),
        space=pltpu.HBM,
        scratch=[pltpu.VMEM(x.shape, x.dtype) for x in inputs]
        + [pltpu.SemaphoreType.DMA((len(inputs),))],
    )(*[pltpu.with_memory_space_constraint(x, pltpu.HBM) for x in inputs])
    prior_base = turned(base, "sec", 1)

    def table(*shape, kind=BF16):
        return jax.ShapeDtypeStruct(shape, kind)

    square = table(count, edge, edge, kind=F32)
    slim, tall = table(count, 16, edge), table(count, edge, LANES)
    *spectra, message = call(
        spectrum_kernel,
        (square, square, slim, slim, tall, tall, table(length, LANES)),
        7,
        scratch=[pltpu.VMEM((16, wide), F32)],
    )(pixels, dft_cos, dft_sin, peaks[0], base, owner[0].reshape(1, rows), render_row)
    near, cross_re, cross_im = call(
        near_kernel,
        (table(8, LANES, kind=F32), table(count, edge, edge), table(count, edge, edge)),
        9,
    )(prior_base, *spectra[:2], dft_cos, dft_sin, *spectra[2:])

    surfaces = call(surface_kernel, (square,) * 3, 4)(cross_re, cross_im, dft_cos, dft_sin)

    def laid(slots):
        deep = round_up(slots * rows, LANES)
        return (table(rows, deep),) + (table(deep, 2 * LANES),) * 3

    def key_line(slots):
        return pltpu.VMEM((8, round_up(slots * rows, LANES)), F32)

    def stack(slots):
        return pltpu.VMEM((round_up(slots * rows, LANES), 2 * LANES), BF16)

    few = strips == 8
    order = [surfaces[0]]
    if few:
        offsets = [2 * k for k in range(strips // 2)]
        blocks = [message]
        for offset in offsets[1:]:
            far = 1 << offset.bit_length() - 1
            blocks.append(swapped(message, far) if offset == far else swapped(blocks[far // 2], offset - far))

        def prepared(group, after):
            return call(
                functools.partial(prepare_kernel, count, edge, len(group)),
                laid(len(group)),
                len(group) + 1,
                scratch=[key_line(len(group))],
            )(*group, after)

        early_side = prepared([message, swapped(message, 1)], near)
        order.append(early_side[0])

    nears = [near] + [turned(near, "sec", k) for k in range(1, sections - 1)]
    patches_all = round_up(count * strips, LANES)
    smooth, prior = call(
        functools.partial(chain_kernel, count, len(nears)),
        (table(8, patches_all, kind=F32), table(8, LANES, kind=F32)),
        len(nears) + len(order),
    )(*nears, *order)
    corr_map, passed = call(map_kernel, (square, table(8, patches_all, kind=F32)), 5)(
        *surfaces, prior, smooth
    )

    rendered = table(edge, rows)
    if few:
        total = sum([swapped(smooth, offset) for offset in offsets[1:]], passed)
        late_side = prepared(blocks[1:] + [swapped(block, 1) for block in blocks[1:]], total)
        groups = [0, 1], offsets[1:] + [offset + 1 for offset in offsets[1:]]
        render = call(
            functools.partial(render_kernel, count, edge, groups),
            rendered,
            10,
            scratch=[stack(len(group)) for group in groups],
        )(*early_side, *late_side, total, swapped(total, 1))
    else:
        render = call(
            functools.partial(render_all_kernel, count, edge),
            rendered,
            2,
            scratch=[pltpu.VMEM(x.shape, x.dtype) for x in laid(1)] + [key_line(1), stack(1)],
            vmem=2 * strips * length * LANES * 2 + VMEM_BYTES,
        )(lax.all_gather(message, "strip"), lax.psum(passed, "strip"))
    return (render.T[None], corr_map[None])


def solution(mesh):
    placed = (
        P("sec", "strip", None, None),
        P("sec", "strip", None),
        P("sec", "strip", None),
        P("sec", "strip", None),
        P("sec", "strip", None),
        P("sec", "strip", None),
        P("sec", "strip", None),
        P("sec", "strip"),
    )
    return jax.shard_map(
        on_device,
        mesh=mesh,
        in_specs=placed,
        out_specs=(P("sec", "strip", None), P("sec", "strip", None, None)),
        check_vma=False,
    )
```
